256 devices in a mesh: doc: 16 (over x, y_lo, core), seq: 16 (over z, y_hi).
Axes of the slice: x: 4, y: 4 (y_hi: 2, y_lo: 2; y = y_hi * 2 + y_lo), z: 8, core: 2. Of those that a mesh axis runs over, the one named last changes fastest.
Arguments:
- doc_query: bfloat16 [16, 4096, 2048], P('doc', 'seq'), may hold values from -6 to 6
- doc_keyval: bfloat16 [16, 2, 4096, 512], P('doc', None, 'seq'), may hold values from -6 to 6
- qry_query: bfloat16 [512, 512, 2048], P(('doc', 'seq')), may hold values from -6 to 6
- qry_keyval: bfloat16 [512, 2, 512, 512], P(('doc', 'seq')), may hold values from -6 to 6
- doc_len: int32 [16], P('doc'), may hold values from 1024 to 4096, as said below
- qry_len: int32 [512], P(('doc', 'seq')), may hold values from 128 to 512, as said below
- positive: int32 [512], P(('doc', 'seq')), may hold values from 0 to 15
Outputs:
- doc_out: bfloat16 [16, 4096, 2048], P('doc', 'seq')
- qry_out: bfloat16 [512, 512, 2048], P(('doc', 'seq'))
- doc_grad: float32 [16, 2048], P('doc')
- query_grad: float32 [512, 2048], P(('doc', 'seq'))
The draws below stay inside these ranges and needn't reach their ends.
Inputs may be any that keep to these rules, and one draw needn't show every extreme that they name: `doc_len`: some document has exactly 4096 live tokens and some exactly 1024. `qry_len`: some query has exactly 512 live tokens and some exactly 128.
All inputs are finite; a program needn't handle non-finite values.
Results may differ from the reference program's by a relative error of at most 0.0095.
Values may be sent and summed in bfloat16 or wider, within the bound.
No kernel may reach another device: no remote copies, remote signals or barrier semaphores. Data moves between devices by JAX's collectives and lax.ppermute only.
A program may use at most 192 MiB of HBM per device.

```python
import math
import jax
import jax.numpy as jnp
from jax import lax

HEADS = 16
KV_HEADS = 4
HEAD_DIM = 128
QLEN = 512
GROUP = 4
EMB = 2048
SEQ = 4096
DOCS = 16
QUERIES = 512


def ragged_lengths(key, count, longest):
    key = jax.random.fold_in(key, 11)
    first, second = jax.random.split(key)
    values = jax.random.randint(first, (count,), longest // 4, longest + 1)
    order = jax.random.permutation(second, count)
    values = values.at[order[0]].set(longest)
    values = values.at[order[1]].set(longest // 4)
    return values.astype(jnp.int32)


def planted_layout(key, salt, count, length, kv_heads, head_dim):
    key = jax.random.fold_in(key, salt)
    parts = jax.random.split(key, 4)
    width = length // 8
    offset = jax.random.randint(parts[0], (count, 2), 0, width - 1)
    key_place = jnp.arange(2)[None, :] * width + offset
    stretch = (length - length // 4) // 4
    query_place = length // 4 + jnp.arange(4)[None, :] * stretch + jax.random.randint(parts[1], (count, 4), 0, stretch)
    signs = jnp.where(jax.random.bernoulli(parts[2], 0.5, (count, 2, kv_heads, head_dim)), 1.0, -1.0).astype(jnp.float32)
    choose = jax.random.randint(parts[3], (count,), 0, 3)
    lower = jnp.where(choose == 0, 110.0, jnp.where(choose == 1, 150.0, 190.0)).astype(jnp.float32)
    target = jnp.stack([lower, jnp.full((count,), 240.0, jnp.float32)], 1)
    root = math.sqrt(head_dim)
    strength = jnp.minimum((target * root / 6.0 - 6.0) / (head_dim - 1), 6.0)
    return (key_place, query_place, signs, strength)


def plant_keys(base, key_place, signs, strength):
    count = base.shape[0]
    length = base.shape[2]
    head_dim = signs.shape[3]
    width = signs.shape[2] * head_dim
    column = jnp.arange(width) % head_dim
    place = jnp.arange(length)
    delta = 2.0 * math.sqrt(head_dim) / 6.0
    keys = base[:, 0]
    for pair in range(2):
        sign_row = signs[:, pair].reshape(count, width)
        pattern = jnp.where(column[None, :] == 1, 6.0, strength[:, pair, None]) * sign_row
        second = jnp.where(column[None, :] == 0, pattern - delta * sign_row, pattern)
        at_first = place[None, :] == key_place[:, pair, None]
        at_second = place[None, :] == key_place[:, pair, None] + 1
        keys = jnp.where(at_first[:, :, None], pattern[:, None, :], keys)
        keys = jnp.where(at_second[:, :, None], second[:, None, :], keys)
    return jnp.stack([keys, base[:, 1]], 1)


def plant_queries(base, query_place, signs, group):
    count, length, width = base.shape
    place = jnp.arange(length)
    rows = base
    for index in range(4):
        pattern = jnp.broadcast_to(signs[:, index // 2, :, None, :], (count, signs.shape[2], group, signs.shape[3])).reshape(count, width)
        at_row = place[None, :] == query_place[:, index, None]
        rows = jnp.where(at_row[:, :, None], 6.0 * pattern[:, None, :], rows)
    return rows


def draw_doc_query(key, part):
    key_place, query_place, signs, strength = planted_layout(key, 41, DOCS, SEQ, KV_HEADS, HEAD_DIM)
    key = jax.random.fold_in(key, 3)
    shape = (DOCS, SEQ, HEADS * HEAD_DIM)
    base = jax.random.truncated_normal(key, -6.0, 6.0, shape, jnp.float32)
    return plant_queries(base, query_place, signs, HEADS // KV_HEADS).astype(jnp.bfloat16)


def draw_doc_keyval(key, part):
    key_place, query_place, signs, strength = planted_layout(key, 41, DOCS, SEQ, KV_HEADS, HEAD_DIM)
    key = jax.random.fold_in(key, 5)
    shape = (DOCS, 2, SEQ, KV_HEADS * HEAD_DIM)
    base = jax.random.truncated_normal(key, -6.0, 6.0, shape, jnp.float32)
    return plant_keys(base, key_place, signs, strength).astype(jnp.bfloat16)


def draw_qry_query(key, part):
    key_place, query_place, signs, strength = planted_layout(key, 43, QUERIES, QLEN, KV_HEADS, HEAD_DIM)
    key = jax.random.fold_in(key, 7)
    shape = (QUERIES, QLEN, HEADS * HEAD_DIM)
    base = jax.random.truncated_normal(key, -6.0, 6.0, shape, jnp.float32)
    return plant_queries(base, query_place, signs, HEADS // KV_HEADS).astype(jnp.bfloat16)


def draw_qry_keyval(key, part):
    key_place, query_place, signs, strength = planted_layout(key, 43, QUERIES, QLEN, KV_HEADS, HEAD_DIM)
    key = jax.random.fold_in(key, 9)
    shape = (QUERIES, 2, QLEN, KV_HEADS * HEAD_DIM)
    base = jax.random.truncated_normal(key, -6.0, 6.0, shape, jnp.float32)
    return plant_keys(base, key_place, signs, strength).astype(jnp.bfloat16)


def draw_doc_len(key, part):
    key = jax.random.fold_in(key, 13)
    return ragged_lengths(key, DOCS, SEQ)


def draw_qry_len(key, part):
    key = jax.random.fold_in(key, 17)
    return ragged_lengths(key, QUERIES, QLEN)


def set_ends(array, rng, least, high):
    index_at = [jax.random.randint(jax.random.fold_in(rng, axis), (), 0, length) for axis, length in enumerate(array.shape)]
    widest = array.shape.index(max(array.shape))
    neighbour = index_at[:widest] + [(index_at[widest] + 1) % array.shape[widest]] + index_at[widest + 1:]
    return array.at[tuple(index_at)].set(least).at[tuple(neighbour)].set(high)


def setup_inputs(seed: int = 0) -> dict:
    arg_keys = jax.random.split(jax.random.key(seed), 8)
    doc_query = draw_doc_query(jax.random.fold_in(arg_keys[7], 71), 0)
    doc_keyval = draw_doc_keyval(jax.random.fold_in(arg_keys[7], 71), 0)
    qry_query = draw_qry_query(jax.random.fold_in(arg_keys[7], 71), 0)
    qry_keyval = draw_qry_keyval(jax.random.fold_in(arg_keys[7], 71), 0)
    doc_len = draw_doc_len(jax.random.fold_in(arg_keys[7], 71), 0)
    qry_len = draw_qry_len(jax.random.fold_in(arg_keys[7], 71), 0)
    positive = set_ends(jax.random.randint(arg_keys[6], (QUERIES,), 0, DOCS), jax.random.fold_in(arg_keys[6], 1), 0, DOCS - 1).astype(jnp.int32)
    return {"doc_query": doc_query, "doc_keyval": doc_keyval, "qry_query": qry_query, "qry_keyval": qry_keyval, "doc_len": doc_len, "qry_len": qry_len, "positive": positive}


def attend(query, keyval, limit):
    count = query.shape[0]
    grouped = jnp.moveaxis(query.reshape(count, KV_HEADS, GROUP, HEAD_DIM), 1, 0)
    keys = jnp.moveaxis(keyval[0].reshape(count, KV_HEADS, HEAD_DIM), 1, 0)
    values = jnp.moveaxis(keyval[1].reshape(count, KV_HEADS, HEAD_DIM), 1, 0)
    place = jnp.arange(count)
    mask = (place[None, :] <= place[:, None]) & (place[None, :] < limit)

    def one_head(operands):
        q_part, k_part, v_part = operands
        scores = jnp.einsum('tgd,sd->gts', q_part.astype(jnp.float32), k_part.astype(jnp.float32)) / HEAD_DIM ** 0.5
        scores = jnp.where(mask[None], scores, -1e+30)
        top = lax.optimization_barrier(jnp.max(scores, -1, keepdims=True))
        expo = jnp.where(mask[None], jnp.exp(scores - top), 0.0)
        total = lax.optimization_barrier(jnp.sum(expo, -1))
        weights = expo.astype(jnp.bfloat16).astype(jnp.float32)
        mixed = jnp.einsum('gts,sd->gtd', weights, v_part.astype(jnp.float32))
        return mixed / total[..., None]
    outputs = lax.map(one_head, (grouped, keys, values))
    return jnp.transpose(outputs, (2, 0, 1, 3)).reshape(count, EMB).astype(jnp.bfloat16)

def contrast(qry_emb, doc_emb, positive, count):
    qnorm = qry_emb * lax.rsqrt(lax.optimization_barrier(jnp.sum(qry_emb * qry_emb, -1, keepdims=True)) + 1e-06)
    dnorm = doc_emb * lax.rsqrt(lax.optimization_barrier(jnp.sum(doc_emb * doc_emb, -1, keepdims=True)) + 1e-06)
    logits = jnp.dot(qnorm, dnorm.T, precision=lax.Precision.HIGHEST) / 0.05
    spread = jnp.log(lax.optimization_barrier(jnp.sum(jnp.exp(logits), -1)))
    picked = jnp.arange(logits.shape[1])[None, :] == positive[:, None]
    chosen = lax.optimization_barrier(jnp.sum(jnp.where(picked, logits, 0.0), -1))
    return jnp.sum(spread - chosen) / count

def reference(doc_query, doc_keyval, qry_query, qry_keyval, doc_len, qry_len, positive):

    def one_sequence(operands):
        query, keyval, limit = operands
        output = attend(query, keyval, limit)
        row = lax.dynamic_slice_in_dim(output, (limit - 1).astype(jnp.int32), 1, 0)
        return (output, row[0])
    doc_out, doc_emb = lax.map(one_sequence, (doc_query, doc_keyval, doc_len))
    qry_out, qry_emb = lax.map(one_sequence, (qry_query, qry_keyval, qry_len))
    count = jnp.float32(QUERIES)

    def loss_of(q_in, d_in):
        return contrast(q_in, d_in, positive, count)
    loss, pullback = jax.vjp(loss_of, qry_emb.astype(jnp.float32), doc_emb.astype(jnp.float32))
    query_grad, doc_grad = pullback(jnp.ones_like(loss))
    return (doc_out, qry_out, doc_grad, query_grad)
```

```python
import functools
import math

import jax
import jax.numpy as jnp
from jax import lax
from jax.experimental import pallas as pl
from jax.experimental.pallas import tpu as pltpu
from jax.sharding import PartitionSpec as P

HEAD = 128
GROUP = 4
TILE = 256
LOW = -1e30
SCALE = math.log2(math.e) / math.sqrt(HEAD)
VMEM = 60 * 2**20
RING = 8


def dot_nt(a, b):
    return lax.dot_general(
        a, b, (((1,), (1,)), ((), ())), preferred_element_type=jnp.float32
    )


def dot_nn(a, b, precision=None):
    return lax.dot_general(
        a, b, (((1,), (0,)), ((), ())), preferred_element_type=jnp.float32, precision=precision
    )


def dot_tn(a, b, precision=None):
    return lax.dot_general(
        a, b, (((0,), (0,)), ((), ())), preferred_element_type=jnp.float32, precision=precision
    )


def pick(rows, target):
    hot = lax.broadcasted_iota(jnp.int32, (8, rows.shape[0]), 1) == target
    return dot_nn(hot.astype(jnp.bfloat16), rows)


def query_kernel(index, len_ref, q_ref, kv_ref, *refs):
    o_ref, e_ref = refs[-2:]
    length = len_ref[index]
    count = q_ref.shape[0]
    heads = q_ref.shape[1] // HEAD
    ones = jnp.ones((count, HEAD), jnp.bfloat16)
    items = [(r, h) for r in range(0, count, TILE) for h in range(heads)]

    def score(r, h):
        g = h // GROUP
        q = q_ref[r : r + TILE, h * HEAD : (h + 1) * HEAD]
        return dot_nt(q, kv_ref[0, : r + TILE, g * HEAD : (g + 1) * HEAD])

    current = score(*items[0])
    for i, (r, h) in enumerate(items):
        following = score(*items[i + 1]) if i + 1 < len(items) else None
        width = r + TILE
        g = h // GROUP
        edge = jnp.minimum(r + lax.broadcasted_iota(jnp.int32, (TILE, 1), 0), length - 1)
        mask = lax.broadcasted_iota(jnp.int32, (TILE, width), 1) <= edge
        s = jnp.where(mask, current, LOW)
        top = jnp.max(s, axis=1, keepdims=True)
        p = jnp.exp2((s - top) * SCALE).astype(jnp.bfloat16)
        v = kv_ref[1, :width, g * HEAD : (g + 1) * HEAD]
        mixed = dot_nn(p, jnp.concatenate([v, ones[:width]], 1))
        out = mixed[:, :HEAD] / mixed[:, HEAD:]
        o_ref[r : r + TILE, h * HEAD : (h + 1) * HEAD] = out.astype(jnp.bfloat16)
        current = following
    e_ref[...] = pick(o_ref[...], length - 1)


def query_attention(lengths, query, keyval, index, previous):
    _, count, emb = query.shape
    parts = 2
    width = emb // parts
    kv_width = keyval.shape[3] // parts
    in_specs = [
        pl.BlockSpec((None, count, width), lambda j, *_: (index, 0, j)),
        pl.BlockSpec((None, 2, count, kv_width), lambda j, *_: (index, 0, 0, j)),
    ]
    args = [lengths, query, keyval]
    alias = {}
    if previous is not None:
        in_specs.append(pl.BlockSpec(memory_space=pl.ANY))
        args.append(previous)
        alias = {3: 0}
    return pl.pallas_call(
        functools.partial(query_kernel, index),
        grid_spec=pltpu.PrefetchScalarGridSpec(
            num_scalar_prefetch=1,
            grid=(parts,),
            in_specs=in_specs,
            out_specs=[
                pl.BlockSpec((None, count, width), lambda j, *_: (index, 0, j)),
                pl.BlockSpec((8, width), lambda j, *_: (0, j)),
            ],
        ),
        out_shape=[
            jax.ShapeDtypeStruct(query.shape, jnp.bfloat16),
            jax.ShapeDtypeStruct((8, emb), jnp.float32),
        ],
        input_output_aliases=alias,
        compiler_params=pltpu.CompilerParams(vmem_limit_bytes=VMEM),
        cost_estimate=pl.CostEstimate(
            flops=4 * count * count * emb, bytes_accessed=5 * 2**20, transcendentals=count * count * 16
        ),
        name="query_attention",
    )(*args)


def doc_kernel(first, last, pairs, places, *refs):
    refs = list(refs)
    q_ref = refs.pop(0)
    blocks = [(refs.pop(0), refs.pop(0)) for _ in range(pairs)]
    if not first:
        ml_in, acc_in = refs.pop(0), refs.pop(0)
    if last:
        o_ref, e_ref = refs
    else:
        ml_out, acc_out = refs
    piece = pl.program_id(1)
    chunk, half, limit = places[0], places[1], places[2]
    span = 2 * TILE
    base = chunk * span + jnp.where(piece == 0, half, 1 - half) * TILE

    def finish(h, low, total, accum):
        columns = slice(h * HEAD, (h + 1) * HEAD)
        if last:
            o_ref[:, columns] = (accum / total).astype(jnp.bfloat16)
        else:
            ml_out[:, h : h + 1] = low
            ml_out[:, 8 + h : 9 + h] = total
            acc_out[:, columns] = accum

    def state(h):
        columns = slice(h * HEAD, (h + 1) * HEAD)
        return ml_in[:, h : h + 1], ml_in[:, 8 + h : 9 + h], acc_in[:, columns]

    def update(used):
        lane = lax.broadcasted_iota(jnp.int32, (1, TILE), 1)
        starts = []
        for n in range(used):
            number = places[3 + n]
            starts += [number * span + half * TILE, number * span + (1 - half) * TILE]
        spots = jnp.concatenate([lane + s for s in starts], 1)
        keys = jnp.concatenate([b[0] for pair in blocks[:used] for b in pair], 0)
        values = jnp.concatenate([b[1] for pair in blocks[:used] for b in pair], 0)
        values = jnp.concatenate([values, jnp.ones_like(values)], 1)
        if first:
            edge = jnp.minimum(base + lax.broadcasted_iota(jnp.int32, (TILE, 1), 0), limit - 1)
            mask = spots <= edge
        else:
            mask = spots < limit

        def score(h):
            return dot_nt(q_ref[:, h * HEAD : (h + 1) * HEAD], keys)

        current = score(0)
        for h in range(GROUP):
            following = score(h + 1) if h + 1 < GROUP else None
            s = jnp.where(mask, current, LOW)
            top = jnp.max(s, axis=1, keepdims=True)
            if not first:
                old_top, old_total, old_accum = state(h)
                top = jnp.maximum(top, old_top)
            p = jnp.exp2((s - top) * SCALE).astype(jnp.bfloat16)
            mixed = dot_nn(p, values)
            accum, total = mixed[:, :HEAD], mixed[:, HEAD : HEAD + 1]
            if not first:
                factor = jnp.exp2((old_top - top) * SCALE)
                accum = accum + old_accum * factor
                total = total + old_total * factor
            finish(h, top, total, accum)
            current = following

    def keep():
        for h in range(GROUP):
            if first:
                finish(h, jnp.full((TILE, 1), LOW), jnp.zeros((TILE, 1)), jnp.zeros((TILE, HEAD)))
            else:
                finish(h, *state(h))

    def useful(n):
        number = places[3 + n]
        return (number >= 0) & (number * span < limit)

    if pairs == 2:
        both = useful(1)
        only = useful(0) & jnp.logical_not(both)
        pl.when(both)(lambda: update(2))
        pl.when(only)(lambda: update(1))
        pl.when(jnp.logical_not(both | only))(keep)
    else:
        pl.when(useful(0))(lambda: update(1))
        pl.when(jnp.logical_not(useful(0)))(keep)
    if last:
        target = limit - 1 - base
        row = pick(o_ref[...], target)

        @pl.when(piece == 0)
        def _():
            e_ref[...] = row

        @pl.when(piece == 1)
        def _():
            e_ref[...] += row


def doc_step(places, query, blocks, carry, last):
    first = carry is None
    pairs = len(blocks) // 2
    _, rows, width = query.shape
    kv_heads = width // (GROUP * HEAD)
    block = GROUP * HEAD
    row_spec = pl.BlockSpec((None, rows, block), lambda g, i, *_: (i, 0, g))
    kv_spec = pl.BlockSpec((2, rows, HEAD), lambda g, i, *_: (0, 0, g))
    ml_spec = pl.BlockSpec((None, None, rows, HEAD), lambda g, i, *_: (g, i, 0, 0))
    in_specs = [row_spec] + [kv_spec] * len(blocks)
    args = [places, query, *blocks]
    alias = {}
    if not first:
        in_specs += [ml_spec, row_spec]
        if not last:
            alias = {len(args): 0, len(args) + 1: 1}
        args += list(carry)
    if last:
        out_specs = [row_spec, pl.BlockSpec((8, block), lambda g, i, *_: (0, g))]
        out_shape = [
            jax.ShapeDtypeStruct(query.shape, jnp.bfloat16),
            jax.ShapeDtypeStruct((8, width), jnp.float32),
        ]
    else:
        out_specs = [ml_spec, row_spec]
        out_shape = [
            jax.ShapeDtypeStruct((kv_heads, 2, rows, HEAD), jnp.float32),
            jax.ShapeDtypeStruct(query.shape, jnp.float32),
        ]
    return pl.pallas_call(
        functools.partial(doc_kernel, first, last, pairs),
        grid_spec=pltpu.PrefetchScalarGridSpec(
            num_scalar_prefetch=1,
            grid=(kv_heads, 2),
            in_specs=in_specs,
            out_specs=out_specs,
        ),
        out_shape=out_shape,
        input_output_aliases=alias,
        compiler_params=pltpu.CompilerParams(vmem_limit_bytes=VMEM),
        cost_estimate=pl.CostEstimate(
            flops=pairs * 4 * 2 * rows * 2 * rows * width, bytes_accessed=6 * 2**20, transcendentals=2**21
        ),
        name="doc_step",
    )(*args)


def contrast_kernel(count, own, q_ref, pos_ref, d_ref, qg_ref, part_ref):
    high = lax.Precision.HIGHEST
    q = q_ref[...]
    d = d_ref[...]
    q_scale = lax.rsqrt(jnp.sum(q * q, axis=1, keepdims=True) + 1e-6)
    d_scale = lax.rsqrt(jnp.sum(d * d, axis=1, keepdims=True) + 1e-6)
    qn = q * q_scale
    dn = d * d_scale
    logits = (
        lax.dot_general(
            qn, dn, (((1,), (1,)), ((), ())), preferred_element_type=jnp.float32, precision=high
        )
        / 0.05
    )
    top = jnp.max(logits, axis=1, keepdims=True)
    expo = jnp.exp(logits - top)
    share = expo / jnp.sum(expo, axis=1, keepdims=True)
    docs = lax.broadcasted_iota(jnp.int32, logits.shape, 1).astype(jnp.float32)
    slope = (share - jnp.where(docs == pos_ref[:, :1], 1.0, 0.0)) * (20.0 / count)
    part_ref[...] = dot_tn(slope, qn, high)
    q_slope = dot_nn(slope[:own], dn, high)
    along = jnp.sum(q_slope * qn[:own], axis=1, keepdims=True)
    qg_ref[...] = (q_slope - qn[:own] * along) * q_scale[:own]


def contrast(count, own, queries, positive, docs):
    whole = pl.BlockSpec(memory_space=pltpu.VMEM)
    return pl.pallas_call(
        functools.partial(contrast_kernel, count, own),
        in_specs=[whole] * 3,
        out_specs=[whole] * 2,
        out_shape=[
            jax.ShapeDtypeStruct((own, queries.shape[1]), jnp.float32),
            jax.ShapeDtypeStruct(docs.shape, jnp.float32),
        ],
        compiler_params=pltpu.CompilerParams(vmem_limit_bytes=VMEM),
        name="contrast",
    )(queries, positive, docs)


def project_kernel(parts_ref, d_ref, o_ref):
    slope = jnp.sum(parts_ref[...], axis=0)
    d = d_ref[...]

    def whole(x):
        return jnp.sum(jnp.sum(x, axis=1, keepdims=True), axis=0, keepdims=True)

    scale = lax.rsqrt(whole(d * d) + 1e-6)
    dn = d * scale
    o_ref[...] = (slope - dn * whole(slope * dn)) * scale


def project(parts, d):
    whole = pl.BlockSpec(memory_space=pltpu.VMEM)
    return pl.pallas_call(
        project_kernel,
        in_specs=[whole] * 2,
        out_specs=whole,
        out_shape=jax.ShapeDtypeStruct(d.shape, jnp.float32),
        name="project",
    )(parts, d)


def along(array, pairs):
    both = [(2 * s + y, 2 * t + y) for s, t in pairs for y in range(2)]
    return lax.ppermute(array, "seq", both)


def across(array):
    return lax.ppermute(array, "seq", [(i, i ^ 1) for i in range(2 * RING)])


def up_pairs(step):
    return [(s, s + 1) for s in range(step - 1, RING - 1)]


def down_pairs(step, hops):
    return [((c - step + 1) % RING, (c - step) % RING) for c in range(hops)]


def shards(doc_query, doc_keyval, qry_query, qry_keyval, doc_len, qry_len, positive):
    rows, emb = doc_query.shape[1:]
    half_emb = emb // 2
    kv_width = doc_keyval.shape[3]
    half_kv = kv_width // 2
    seq_count = lax.axis_size("seq")
    doc_count = lax.axis_size("doc")
    seq_index = lax.axis_index("seq")
    half = lax.rem(seq_index, 2)
    chunk = seq_index // 2
    limit = doc_len[0]

    def columns(array, which, width):
        axis = array.ndim - 1
        return lax.dynamic_slice_in_dim(array, which * width, width, axis)

    keyval = doc_keyval[0]
    near = columns(keyval, half, half_kv)
    far = across(columns(keyval, 1 - half, half_kv))
    own_rows = columns(doc_query[0], half, half_emb)
    query = jnp.stack([own_rows, across(columns(doc_query[0], 1 - half, half_emb))])

    qry_out, first_row = query_attention(qry_len, qry_query, qry_keyval, 0, None)
    qry_out, second_row = query_attention(qry_len, qry_query, qry_keyval, 1, qry_out)
    own = qry_query.shape[0]
    held = jnp.concatenate(
        [
            jnp.concatenate([first_row[:1], second_row[:1]], 0),
            jnp.broadcast_to(positive.astype(jnp.float32)[:, None], (own, HEAD)),
        ],
        1,
    )
    for k in (2, 4, 8, 1):
        held = jnp.concatenate([held, lax.ppermute(held, "seq", [(i, i ^ k) for i in range(2 * RING)])], 0)

    def places(up, down):
        return jnp.stack([chunk, half, limit, up, down]).astype(jnp.int32)

    carry = doc_step(places(chunk, chunk), query, [near, far], None, False)
    up_near, up_far, down_near, down_far = near, far, near, far
    for step in range(1, 5):
        up_near = along(up_near, up_pairs(step))
        if step < 4:
            down_near = along(down_near, down_pairs(step, 3))
            up_far = along(up_far, up_pairs(step))
        down_far = along(down_far, down_pairs(step, 4))
        if step < 4:
            blocks = [up_near, up_far, down_near, down_far]
        else:
            blocks = [up_near, down_far]
        carry = doc_step(
            places(chunk - step, chunk + step - RING), query, blocks, carry, step == 4
        )
    output, row = carry
    other = across(output[1])
    mine = output[0]
    doc_out = jnp.where(
        half == 0, jnp.concatenate([mine, other], 1), jnp.concatenate([other, mine], 1)
    )

    lanes = half_emb // HEAD
    spread = lax.all_to_all(
        jnp.broadcast_to(row[0].reshape(1, lanes, HEAD), (seq_count, lanes, HEAD)), "seq", 0, 0, tiled=True
    )
    pooled = jnp.sum(spread.reshape(RING, 2, lanes, HEAD), 0).reshape(2 * lanes, HEAD)
    docs = lax.all_to_all(
        jnp.broadcast_to(pooled[None], (doc_count, 2 * lanes, HEAD)), "doc", 0, 0, tiled=True
    )
    count = float(own * seq_count * doc_count)
    query_grad, part = contrast(
        count, own, held[:, :emb], held[:, emb:], docs.reshape(doc_count, emb)
    )
    parts = lax.all_to_all(part.reshape(doc_count, 2 * lanes, HEAD), "doc", 0, 0, tiled=True)
    doc_grad = project(parts, pooled).reshape(1, emb)
    return (doc_out[None], qry_out, doc_grad, query_grad)


def solution(mesh):
    placed = (
        P("doc", "seq", None),
        P("doc", None, "seq", None),
        P(("doc", "seq"), None, None),
        P(("doc", "seq"), None, None, None),
        P("doc"),
        P(("doc", "seq")),
        P(("doc", "seq")),
    )
    return jax.shard_map(
        shards,
        mesh=mesh,
        in_specs=placed,
        out_specs=(
            P("doc", "seq", None),
            P(("doc", "seq"), None, None),
            P("doc", None),
            P(("doc", "seq"), None),
        ),
        check_vma=False,
    )
```

```python
import functools
import math

import jax
import jax.numpy as jnp
from jax import lax
from jax.experimental import pallas as pl
from jax.experimental.pallas import tpu as pltpu
from jax.sharding import PartitionSpec as P

HEAD = 128
GROUP = 4
TILE = 256
LOW = -1e30
SCALE = math.log2(math.e) / math.sqrt(HEAD)
VMEM = 60 * 2**20
RING = 8
EXTRA = 32
LABEL = 4
HEADS_HALF = 8


def dot_nt(a, b):
    return lax.dot_general(
        a, b, (((1,), (1,)), ((), ())), preferred_element_type=jnp.float32
    )


def dot_nn(a, b, precision=None):
    return lax.dot_general(
        a, b, (((1,), (0,)), ((), ())), preferred_element_type=jnp.float32, precision=precision
    )


def dot_tn(a, b, precision=None):
    return lax.dot_general(
        a, b, (((0,), (0,)), ((), ())), preferred_element_type=jnp.float32, precision=precision
    )


def query_kernel(index, len_ref, q_ref, kv_ref, *refs):
    o_ref = refs[-1]
    length = len_ref[index]
    count = q_ref.shape[0]
    heads = q_ref.shape[1] // HEAD
    ones = jnp.ones((count, HEAD), jnp.bfloat16)
    items = [(r, h) for r in range(0, count, TILE) for h in range(heads)]

    def score(r, h):
        g = h // GROUP
        q = q_ref[r : r + TILE, h * HEAD : (h + 1) * HEAD]
        return dot_nt(q, kv_ref[0, : r + TILE, g * HEAD : (g + 1) * HEAD])

    current = score(*items[0])
    for i, (r, h) in enumerate(items):
        following = score(*items[i + 1]) if i + 1 < len(items) else None
        width = r + TILE
        g = h // GROUP
        edge = jnp.minimum(r + lax.broadcasted_iota(jnp.int32, (TILE, 1), 0), length - 1)
        mask = lax.broadcasted_iota(jnp.int32, (TILE, width), 1) <= edge
        s = jnp.where(mask, current, LOW)
        top = jnp.max(s, axis=1, keepdims=True)
        p = jnp.exp2((s - top) * SCALE).astype(jnp.bfloat16)
        v = kv_ref[1, :width, g * HEAD : (g + 1) * HEAD]
        mixed = dot_nn(p, jnp.concatenate([v, ones[:width]], 1))
        out = mixed[:, :HEAD] / mixed[:, HEAD:]
        o_ref[r : r + TILE, h * HEAD : (h + 1) * HEAD] = out.astype(jnp.bfloat16)
        current = following


def query_attention(lengths, query, keyval, index, previous):
    _, count, emb = query.shape
    parts = 2
    width = emb // parts
    kv_width = keyval.shape[3] // parts
    in_specs = [
        pl.BlockSpec((None, count, width), lambda j, *_: (index, 0, j)),
        pl.BlockSpec((None, 2, count, kv_width), lambda j, *_: (index, 0, 0, j)),
    ]
    args = [lengths, query, keyval]
    alias = {}
    if previous is not None:
        in_specs.append(pl.BlockSpec(memory_space=pl.ANY))
        args.append(previous)
        alias = {3: 0}
    return pl.pallas_call(
        functools.partial(query_kernel, index),
        grid_spec=pltpu.PrefetchScalarGridSpec(
            num_scalar_prefetch=1,
            grid=(parts,),
            in_specs=in_specs,
            out_specs=pl.BlockSpec((None, count, width), lambda j, *_: (index, 0, j)),
        ),
        out_shape=jax.ShapeDtypeStruct(query.shape, jnp.bfloat16),
        input_output_aliases=alias,
        compiler_params=pltpu.CompilerParams(vmem_limit_bytes=VMEM),
        cost_estimate=pl.CostEstimate(
            flops=4 * count * count * emb, bytes_accessed=5 * 2**20, transcendentals=count * count * 16
        ),
        name="query_attention",
    )(*args)


def row_attention(row, kv_ref, which, length, heads):
    stacked = jnp.concatenate([row[:, h * HEAD : (h + 1) * HEAD] for h in range(heads)], 0)
    group = lax.broadcasted_iota(jnp.int32, (heads, 1), 0) // GROUP
    count = kv_ref.shape[2]
    s = jnp.zeros((heads, count), jnp.float32)
    for g in range(heads // GROUP):
        keys = kv_ref[which, 0, :, g * HEAD : (g + 1) * HEAD]
        s = jnp.where(group == g, dot_nt(stacked, keys), s)
    s = jnp.where(lax.broadcasted_iota(jnp.int32, (1, count), 1) < length, s, LOW)
    p = jnp.exp2((s - jnp.max(s, axis=1, keepdims=True)) * SCALE)
    total = jnp.sum(p, axis=1, keepdims=True)
    p = p.astype(jnp.bfloat16)
    mixed = jnp.zeros((heads, HEAD), jnp.float32)
    for g in range(heads // GROUP):
        values = kv_ref[which, 1, :, g * HEAD : (g + 1) * HEAD]
        mixed = jnp.where(group == g, dot_nn(p, values), mixed)
    return (mixed / total).astype(jnp.bfloat16)


def pack_kernel(places, q_near, q_far, kv_near, kv_far, first_ref, second_ref, qkv_ref, near_ref, send_ref, q_out):
    chunk, half, limit = places[0], places[1], places[2]
    rows = q_near.shape[0]
    width = kv_near.shape[2]
    lines = width // HEAD
    q_out[...] = q_far[...]
    row = limit - 1 - (2 * chunk + half) * rows
    shape = (EXTRA // 2, rows)
    here = lax.broadcasted_iota(jnp.int32, shape, 1) == row
    line = lax.broadcasted_iota(jnp.int32, shape, 0)
    labels = lax.broadcasted_iota(jnp.int32, (EXTRA // 2, width), 0)
    queries = []
    for e, ref in enumerate((first_ref, second_ref)):
        length = places[3 + e]
        emb = ref.shape[1]
        heads = emb // HEAD
        hot = lax.broadcasted_iota(jnp.int32, (8, ref.shape[0]), 1) == lax.rem(length - 1, ref.shape[0])
        one = dot_nn(hot.astype(jnp.bfloat16), ref[...])[:1].astype(jnp.bfloat16)
        out = row_attention(one, qkv_ref, e, length, heads)
        spot = lax.broadcasted_iota(jnp.int32, (heads // lines, heads), 1)
        want = lax.broadcasted_iota(jnp.int32, (heads // lines, heads), 0) * lines
        parts = [dot_nn((spot == want + j).astype(jnp.bfloat16), out) for j in range(lines)]
        queries.append(jnp.concatenate(parts, 1))
    queries = jnp.concatenate(queries, 0).astype(jnp.bfloat16)
    for q_ref, kv_ref, out_ref in ((q_near, kv_near, near_ref), (q_far, kv_far, send_ref)):
        out_ref[:rows] = kv_ref[0]
        out_ref[rows : 2 * rows] = kv_ref[1]
        found = jnp.zeros((EXTRA // 2, width), jnp.float32)
        for j in range(q_ref.shape[1] // width):
            hot = (here & (line == j)).astype(jnp.bfloat16)
            found += dot_nn(hot, q_ref[:, j * width : (j + 1) * width])
        for e in range(2):
            found = jnp.where(labels == LABEL + e, places[5 + e].astype(jnp.float32), found)
        out_ref[2 * rows : 2 * rows + EXTRA // 2] = found.astype(jnp.bfloat16)
        out_ref[2 * rows + EXTRA // 2 :] = queries


def pack(places, query, keyval, qry_query, qry_keyval):
    rows, emb = query.shape
    width = keyval.shape[2] // 2
    length = 2 * rows + EXTRA
    step = 16
    near = lambda i, p: (0, p[1])
    far = lambda i, p: (0, 1 - p[1])
    return pl.pallas_call(
        pack_kernel,
        grid_spec=pltpu.PrefetchScalarGridSpec(
            num_scalar_prefetch=1,
            grid=(1,),
            in_specs=[
                pl.BlockSpec((rows, emb // 2), near),
                pl.BlockSpec((rows, emb // 2), far),
                pl.BlockSpec((2, rows, width), lambda i, p: (0, 0, p[1])),
                pl.BlockSpec((2, rows, width), lambda i, p: (0, 0, 1 - p[1])),
                pl.BlockSpec((None, step, emb), lambda i, p: (0, (p[3] - 1) // step, 0)),
                pl.BlockSpec((None, step, emb), lambda i, p: (1, (p[4] - 1) // step, 0)),
                pl.BlockSpec(qry_keyval.shape, lambda i, p: (0, 0, 0, 0)),
            ],
            out_specs=[pl.BlockSpec((length, width), lambda i, p: (0, 0))] * 2
            + [pl.BlockSpec((rows, emb // 2), lambda i, p: (0, 0))],
        ),
        out_shape=[jax.ShapeDtypeStruct((length, width), jnp.bfloat16)] * 2
        + [jax.ShapeDtypeStruct((rows, emb // 2), jnp.bfloat16)],
        compiler_params=pltpu.CompilerParams(vmem_limit_bytes=VMEM),
        name="pack",
    )(places, query, query, keyval, keyval, qry_query, qry_query, qry_keyval)


def doc_kernel(final, hops, only, places, *refs):
    if final:
        q_ref, refs = refs[0], refs[1:]
        piece = jnp.int32(only)
    else:
        own_ref, lent_ref, refs = refs[0], refs[1], refs[2:]
        piece = pl.program_id(1)
    blocks = [(refs[2 * n], refs[2 * n + 1]) for n in range(len(hops))]
    refs = refs[2 * len(hops) :]
    if final:
        o_in, lse_in, o_ref, k_ref, v_ref, spot_ref = refs
    else:
        o_ref, lse_ref, k_ref, v_ref, spot_ref, q_ref = refs
    chunk, half, limit = places[0], places[1], places[2]
    rows = q_ref.shape[0]
    span = 2 * rows
    row_half = jnp.where(piece == 0, half, 1 - half)
    base = chunk * span + row_half * rows

    if not final:

        @pl.when(piece == 0)
        def _():
            q_ref[...] = own_ref[...]

        @pl.when(piece == 1)
        def _():
            q_ref[...] = lent_ref[...]

    v_ref[:, HEAD:] = jnp.ones((v_ref.shape[0], HEAD), jnp.bfloat16)
    lane = lax.broadcasted_iota(jnp.int32, (8, rows), 1)
    count = jnp.int32(0)
    for hop, pair in zip(hops, blocks):
        number = lax.rem(chunk - hop + RING, RING)
        need = (number <= chunk) & (number * span < limit)

        @pl.when(need)
        def _(number=number, pair=pair, count=count):
            for side, block in enumerate(pair):
                start = pl.multiple_of(count * span + side * rows, rows)
                k_ref[pl.ds(start, rows)] = block[:rows]
                v_ref[pl.ds(start, rows), :HEAD] = block[rows : 2 * rows]
                place = half if side == 0 else 1 - half
                spot_ref[:, pl.ds(start, rows)] = lane + number * span + place * rows

        count = count + need.astype(jnp.int32)

    def update(used):
        width = used * span
        edge = base + lax.broadcasted_iota(jnp.int32, (rows, 1), 0)
        mask = spot_ref[:1, :width] <= jnp.minimum(edge, limit - 1)

        def score(h):
            return dot_nt(q_ref[:, h * HEAD : (h + 1) * HEAD], k_ref[:width])

        current = score(0)
        for h in range(GROUP):
            columns = slice(h * HEAD, (h + 1) * HEAD)
            following = score(h + 1) if h + 1 < GROUP else None
            s = jnp.where(mask, current, LOW)
            top = jnp.max(s, axis=1, keepdims=True)
            if final:
                before = lse_in[:, columns]
                high = jnp.maximum(before, top * SCALE)
                p = jnp.exp2(s * SCALE - jnp.concatenate([high] * (width // HEAD), 1))
                mixed = dot_nn(p.astype(jnp.bfloat16), v_ref[:width])
                factor = jnp.exp2(before - high)
                out = (o_in[:, columns].astype(jnp.float32) * factor + mixed[:, :HEAD]) / (
                    factor + mixed[:, HEAD:]
                )
            else:
                p = jnp.exp2((s - top) * SCALE)
                mixed = dot_nn(p.astype(jnp.bfloat16), v_ref[:width])
                total = mixed[:, HEAD:]
                out = mixed[:, :HEAD] / total
                lse_ref[:, columns] = top * SCALE + jnp.log2(total)
            o_ref[:, columns] = out.astype(jnp.bfloat16)
            current = following

    for used in range(1, len(hops) + 1):
        pl.when(count == used)(functools.partial(update, used))

    @pl.when(count == 0)
    def _():
        if final:
            o_ref[...] = o_in[...]
        else:
            o_ref[...] = jnp.zeros_like(o_ref)
            lse_ref[...] = jnp.full_like(lse_ref, LOW)


def doc_part(places, query, lent, blocks, hops, before=None, only=None):
    final = before is not None
    rows, width = lent.shape
    block = GROUP * HEAD
    kv_heads = width // block
    length = blocks[0].shape[0]
    span = 2 * rows * len(hops)
    own_spec = pl.BlockSpec((rows, block), lambda g, i, p: (0, p[1] * kv_heads + g))
    row_spec = pl.BlockSpec((rows, block), lambda g, i, p: (0, g))
    kv_spec = pl.BlockSpec((length, HEAD), lambda g, i, p: (0, g))
    scratch = [
        pltpu.VMEM((span, HEAD), jnp.bfloat16),
        pltpu.VMEM((span, 2 * HEAD), jnp.bfloat16),
        pltpu.VMEM((8, span), jnp.int32),
    ]
    if final:
        piece_spec = pl.BlockSpec((None, rows, block), lambda g, i, p: (only, 0, g))
        spec, rows_in = [(own_spec, query), (row_spec, lent)][only]
        in_specs = [spec] + [kv_spec] * len(blocks) + [piece_spec] * 2
        args = [places, rows_in, *blocks, *before]
        out_specs = spec
        out_shape = jax.ShapeDtypeStruct(rows_in.shape, jnp.bfloat16)
    else:
        piece_spec = pl.BlockSpec((None, rows, block), lambda g, i, p: (i, 0, g))
        in_specs = [own_spec, row_spec] + [kv_spec] * len(blocks)
        args = [places, query, lent, *blocks]
        out_specs = [piece_spec] * 2
        out_shape = [
            jax.ShapeDtypeStruct((2, rows, width), jnp.bfloat16),
            jax.ShapeDtypeStruct((2, rows, width), jnp.float32),
        ]
        scratch.append(pltpu.VMEM((rows, block), jnp.bfloat16))
    pieces = 1 if final else 2
    return pl.pallas_call(
        functools.partial(doc_kernel, final, hops, only),
        grid_spec=pltpu.PrefetchScalarGridSpec(
            num_scalar_prefetch=1,
            grid=(kv_heads, pieces),
            in_specs=in_specs,
            out_specs=out_specs,
            scratch_shapes=scratch,
        ),
        out_shape=out_shape,
        compiler_params=pltpu.CompilerParams(vmem_limit_bytes=VMEM),
        cost_estimate=pl.CostEstimate(
            flops=len(hops) * 4 * pieces * rows * 2 * rows * width,
            bytes_accessed=6 * 2**20,
            transcendentals=2**21,
        ),
        name="doc_part",
    )(*args)


def last_row_kernel(places, *refs):
    blocks, o_ref = refs[:-1], refs[-1]
    chunk, half, limit = places[0], places[1], places[2]
    rows = (blocks[0].shape[0] - EXTRA) // 2
    span = 2 * rows
    lane = lax.broadcasted_iota(jnp.int32, (1, rows), 1)
    spots = []
    query = jnp.zeros((EXTRA // 2, blocks[0].shape[1]), jnp.float32)
    for n, block in enumerate(blocks):
        hop, side = n // 2, n % 2
        number = lax.rem(chunk - hop + RING, RING)
        place = jnp.where(side == 0, half, 1 - half)
        spots.append(lane + number * span + place * rows)
        query += block[2 * rows : 2 * rows + EXTRA // 2].astype(jnp.float32)
    mask = jnp.concatenate(spots, 1) < limit
    lines = query.shape[1] // HEAD
    per = HEADS_HALF // lines
    stacked = jnp.concatenate([query[:per, j * HEAD : (j + 1) * HEAD] for j in range(lines)], 0)
    stacked = stacked.astype(jnp.bfloat16)
    line = lax.rem(lax.broadcasted_iota(jnp.int32, (HEADS_HALF, 1), 0), per)
    groups = HEADS_HALF // GROUP
    group = line // (per // groups)
    scores = jnp.zeros((HEADS_HALF, mask.shape[1]), jnp.float32)
    for g in range(groups):
        keys = jnp.concatenate([b[:rows, g * HEAD : (g + 1) * HEAD] for b in blocks], 0)
        scores = jnp.where(group == g, dot_nt(stacked, keys), scores)
    s = jnp.where(mask, scores, LOW)
    top = jnp.max(s, axis=1, keepdims=True)
    p = jnp.exp2((s - top) * SCALE)
    total = jnp.sum(p, axis=1, keepdims=True)
    weights = p.astype(jnp.bfloat16)
    mixed = jnp.zeros((HEADS_HALF, HEAD), jnp.float32)
    for g in range(groups):
        values = jnp.concatenate([b[rows : 2 * rows, g * HEAD : (g + 1) * HEAD] for b in blocks], 0)
        mixed = jnp.where(group == g, dot_nn(weights, values), mixed)
    out = (mixed / total).astype(jnp.bfloat16).astype(jnp.float32)
    ordered = jnp.concatenate(
        [out[(h % lines) * per + h // lines :][:1] for h in range(HEADS_HALF)], 0
    )
    blank = jnp.zeros_like(ordered)
    o_ref[:HEADS_HALF] = jnp.where(half == 0, ordered, blank)
    o_ref[HEADS_HALF:] = jnp.where(half == 0, blank, ordered)


def last_row(places, blocks):
    whole = pl.BlockSpec(memory_space=pltpu.VMEM)
    return pl.pallas_call(
        last_row_kernel,
        in_specs=[pl.BlockSpec(memory_space=pltpu.SMEM)] + [whole] * len(blocks),
        out_specs=whole,
        out_shape=jax.ShapeDtypeStruct((2 * HEADS_HALF, HEAD), jnp.float32),
        compiler_params=pltpu.CompilerParams(vmem_limit_bytes=VMEM),
        cost_estimate=pl.CostEstimate(flops=2**25, bytes_accessed=4 * 2**20, transcendentals=2**15),
        name="last_row",
    )(places, *blocks)


def contrast_kernel(count, places, d_ref, *refs):
    blocks = refs[:-4]
    qg_ref, part_ref, label_ref, row_ref = refs[-4:]
    high = lax.Precision.HIGHEST
    sources = len(blocks)
    for n, block in enumerate(blocks):
        label_ref[n] = block[: EXTRA // 2].astype(jnp.float32)
        row_ref[n] = block[EXTRA // 2 :].astype(jnp.float32)
    lines = EXTRA // 4
    q = jnp.concatenate(
        [jnp.concatenate([row_ref[:, e * lines + j, :] for j in range(lines)], 1) for e in range(2)], 0
    )
    label = jnp.concatenate([label_ref[:, LABEL + e, :1] for e in range(2)], 0)
    strips = d_ref.shape[1]
    d = jnp.concatenate([d_ref[:, j, :] for j in range(strips)], 1)
    q_scale = lax.rsqrt(jnp.sum(q * q, axis=1, keepdims=True) + 1e-6)
    d_scale = lax.rsqrt(jnp.sum(d * d, axis=1, keepdims=True) + 1e-6)
    qn = q * q_scale
    dn = d * d_scale
    logits = (
        lax.dot_general(
            qn, dn, (((1,), (1,)), ((), ())), preferred_element_type=jnp.float32, precision=high
        )
        / 0.05
    )
    top = jnp.max(logits, axis=1, keepdims=True)
    expo = jnp.exp(logits - top)
    share = expo / jnp.sum(expo, axis=1, keepdims=True)
    docs = lax.broadcasted_iota(jnp.int32, logits.shape, 1).astype(jnp.float32)
    slope = (share - jnp.where(docs == label, 1.0, 0.0)) * (20.0 / count)
    part = dot_tn(slope, qn, high)
    for j in range(strips):
        part_ref[:, j, :] = part[:, j * HEAD : (j + 1) * HEAD]

    def own(x):
        return jnp.concatenate([x[e * sources : e * sources + 1] for e in range(2)], 0)

    q_slope = dot_nn(own(slope), dn, high)
    along = jnp.sum(q_slope * own(qn), axis=1, keepdims=True)
    qg_ref[...] = (q_slope - own(qn) * along) * own(q_scale)


def contrast(count, places, docs, blocks):
    emb = docs.shape[1] * docs.shape[2]
    length, width = blocks[0].shape
    sources = len(blocks)
    extra = pl.BlockSpec((EXTRA, width), lambda i, p: (length // EXTRA - 1, 0))
    return pl.pallas_call(
        functools.partial(contrast_kernel, count),
        grid_spec=pltpu.PrefetchScalarGridSpec(
            num_scalar_prefetch=1,
            grid=(1,),
            in_specs=[pl.BlockSpec(docs.shape, lambda i, p: (0, 0, 0))] + [extra] * sources,
            out_specs=[
                pl.BlockSpec((2, emb), lambda i, p: (0, 0)),
                pl.BlockSpec(docs.shape, lambda i, p: (0, 0, 0)),
            ],
            scratch_shapes=[pltpu.VMEM((sources, EXTRA // 2, width), jnp.float32)] * 2,
        ),
        out_shape=[
            jax.ShapeDtypeStruct((2, emb), jnp.float32),
            jax.ShapeDtypeStruct(docs.shape, jnp.float32),
        ],
        compiler_params=pltpu.CompilerParams(vmem_limit_bytes=VMEM),
        name="contrast",
    )(places, docs, *blocks)


def project_kernel(parts_ref, d_ref, o_ref):
    slope = jnp.sum(parts_ref[...], axis=0)
    d = d_ref[...]

    def whole(x):
        return jnp.sum(jnp.sum(x, axis=1, keepdims=True), axis=0, keepdims=True)

    scale = lax.rsqrt(whole(d * d) + 1e-6)
    dn = d * scale
    out = (slope - dn * whole(slope * dn)) * scale
    for j in range(d.shape[0]):
        o_ref[:, j * HEAD : (j + 1) * HEAD] = out[j : j + 1]


def project(parts, d):
    whole = pl.BlockSpec(memory_space=pltpu.VMEM)
    return pl.pallas_call(
        project_kernel,
        in_specs=[whole] * 2,
        out_specs=whole,
        out_shape=jax.ShapeDtypeStruct((1, d.shape[0] * d.shape[1]), jnp.float32),
        name="project",
    )(parts, d)


def along(array, pairs):
    both = [(2 * s + y, 2 * t + y) for s, t in pairs for y in range(2)]
    return lax.ppermute(array, "seq", both)


def across(array):
    return lax.ppermute(array, "seq", [(i, i ^ 1) for i in range(2 * RING)])


def ring(step):
    return [(s, (s + step) % RING) for s in range(RING)]


def after(array, *earlier):
    return lax.optimization_barrier((array, *earlier))[0]


def shards(doc_query, doc_keyval, qry_query, qry_keyval, doc_len, qry_len, positive):
    emb = doc_query.shape[2]
    seq_count = lax.axis_size("seq")
    doc_count = lax.axis_size("doc")
    seq_index = lax.axis_index("seq")
    half = lax.rem(seq_index, 2)
    half_emb = emb // 2
    own = qry_query.shape[0]
    places = jnp.concatenate(
        [jnp.stack([seq_index // 2, half]).astype(jnp.int32), doc_len, qry_len, positive]
    )
    near, sent, wanted = pack(places, doc_query[0], doc_keyval[0], qry_query, qry_keyval)
    up_near, down_near, up_far, down_far = {0: near}, {0: near}, {}, {}

    def forward(store, step, way, *earlier):
        store[step] = along(after(store[step - 1], *earlier), ring(way))

    def blocks_of(*pairs):
        return [block for pair in pairs for block in pair]

    forward(up_near, 1, 1)
    forward(down_near, 1, -1)
    far = across(sent)
    up_far[0] = down_far[0] = far
    lent = across(wanted)
    qry_out = query_attention(after(qry_len, near), qry_query, qry_keyval, 0, None)
    forward(up_far, 1, 1, qry_out)
    forward(down_far, 1, -1, qry_out)
    forward(up_near, 2, 1, qry_out)
    forward(down_near, 2, -1, qry_out)
    forward(up_far, 2, 1)
    forward(down_far, 2, -1)
    forward(up_near, 3, 1)
    forward(down_near, 3, -1)
    early = (0, 1, RING - 1)
    partial = doc_part(
        after(places, up_near[2], down_near[2]),
        doc_query[0],
        lent,
        blocks_of((near, far), (up_near[1], up_far[1]), (down_near[1], down_far[1])),
        early,
        None,
    )
    forward(up_far, 3, 1, partial[0])
    forward(down_far, 3, -1, partial[0])
    forward(up_near, 4, 1, partial[0])
    forward(down_far, 4, -1)
    by_hop = [(up_near[n], up_far[n]) for n in range(4)] + [(up_near[4], down_far[4])]
    by_hop += [(down_near[n], down_far[n]) for n in (3, 2, 1)]
    everything = blocks_of(*by_hop)
    row = last_row(after(places, *everything), everything)
    moved = across(row)
    qry_out = query_attention(after(qry_len, row), qry_query, qry_keyval, 1, qry_out)
    pooled = row + after(moved, qry_out)
    docs = lax.all_to_all(
        jnp.broadcast_to(pooled[None], (doc_count, *pooled.shape)), "doc", 0, 0, tiled=True
    )
    count = float(own * seq_count * doc_count)
    query_grad, part = contrast(count, places, docs, everything)
    parts = lax.all_to_all(part, "doc", 0, 0, tiled=True)
    late = (2, 3, 4, 5, 6)
    late_blocks = blocks_of(*(by_hop[n] for n in late))
    loan = doc_part(after(places, part), doc_query[0], lent, late_blocks, late, partial, 1)
    other = across(loan)
    mine = doc_part(after(places, loan), doc_query[0], lent, late_blocks, late, partial, 0)
    doc_out = lax.dynamic_update_slice_in_dim(mine, other, (1 - half) * half_emb, 1)
    doc_grad = project(parts, pooled)
    return (doc_out[None], qry_out, doc_grad, query_grad)


def solution(mesh):
    placed = (
        P("doc", "seq", None),
        P("doc", None, "seq", None),
        P(("doc", "seq"), None, None),
        P(("doc", "seq"), None, None, None),
        P("doc"),
        P(("doc", "seq")),
        P(("doc", "seq")),
    )
    return jax.shard_map(
        shards,
        mesh=mesh,
        in_specs=placed,
        out_specs=(
            P("doc", "seq", None),
            P(("doc", "seq"), None, None),
            P("doc", None),
            P(("doc", "seq"), None),
        ),
        check_vma=False,
    )
```

```python
import functools
import math

import jax
import jax.numpy as jnp
from jax import lax
from jax.experimental import pallas as pl
from jax.experimental.pallas import tpu as pltpu
from jax.sharding import PartitionSpec as P

HEAD = 128
GROUP = 4
TILE = 256
LOW = -1e30
SCALE = math.log2(math.e) / math.sqrt(HEAD)
VMEM = 60 * 2**20
RING = 8
EXTRA = 32
LABEL = 4
HEADS_HALF = 8


def dot_nt(a, b):
    return lax.dot_general(
        a, b, (((1,), (1,)), ((), ())), preferred_element_type=jnp.float32
    )


def dot_nn(a, b, precision=None):
    return lax.dot_general(
        a, b, (((1,), (0,)), ((), ())), preferred_element_type=jnp.float32, precision=precision
    )


def dot_tn(a, b, precision=None):
    return lax.dot_general(
        a, b, (((0,), (0,)), ((), ())), preferred_element_type=jnp.float32, precision=precision
    )


def query_kernel(index, len_ref, q_ref, kv_ref, *refs):
    o_ref = refs[-1]
    length = len_ref[index]
    count = q_ref.shape[0]
    heads = q_ref.shape[1] // HEAD
    ones = jnp.ones((count, HEAD), jnp.bfloat16)
    items = [(r, h) for r in range(0, count, TILE) for h in range(heads)]

    def score(r, h):
        g = h // GROUP
        q = q_ref[r : r + TILE, h * HEAD : (h + 1) * HEAD]
        return dot_nt(q, kv_ref[0, : r + TILE, g * HEAD : (g + 1) * HEAD])

    current = score(*items[0])
    for i, (r, h) in enumerate(items):
        following = score(*items[i + 1]) if i + 1 < len(items) else None
        width = r + TILE
        g = h // GROUP
        edge = jnp.minimum(r + lax.broadcasted_iota(jnp.int32, (TILE, 1), 0), length - 1)
        mask = lax.broadcasted_iota(jnp.int32, (TILE, width), 1) <= edge
        s = jnp.where(mask, current, LOW)
        top = jnp.max(s, axis=1, keepdims=True)
        p = jnp.exp2((s - top) * SCALE).astype(jnp.bfloat16)
        v = kv_ref[1, :width, g * HEAD : (g + 1) * HEAD]
        mixed = dot_nn(p, jnp.concatenate([v, ones[:width]], 1))
        out = mixed[:, :HEAD] / mixed[:, HEAD:]
        o_ref[r : r + TILE, h * HEAD : (h + 1) * HEAD] = out.astype(jnp.bfloat16)
        current = following


def query_attention(lengths, query, keyval, index, previous):
    _, count, emb = query.shape
    parts = 2
    width = emb // parts
    kv_width = keyval.shape[3] // parts
    in_specs = [
        pl.BlockSpec((None, count, width), lambda j, *_: (index, 0, j)),
        pl.BlockSpec((None, 2, count, kv_width), lambda j, *_: (index, 0, 0, j)),
    ]
    args = [lengths, query, keyval]
    alias = {}
    if previous is not None:
        in_specs.append(pl.BlockSpec(memory_space=pl.ANY))
        args.append(previous)
        alias = {3: 0}
    return pl.pallas_call(
        functools.partial(query_kernel, index),
        grid_spec=pltpu.PrefetchScalarGridSpec(
            num_scalar_prefetch=1,
            grid=(parts,),
            in_specs=in_specs,
            out_specs=pl.BlockSpec((None, count, width), lambda j, *_: (index, 0, j)),
        ),
        out_shape=jax.ShapeDtypeStruct(query.shape, jnp.bfloat16),
        input_output_aliases=alias,
        compiler_params=pltpu.CompilerParams(vmem_limit_bytes=VMEM),
        cost_estimate=pl.CostEstimate(
            flops=4 * count * count * emb, bytes_accessed=5 * 2**20, transcendentals=count * count * 16
        ),
        name="query_attention",
    )(*args)


def row_attention(row, kv_ref, which, length, heads):
    stacked = jnp.concatenate([row[:, h * HEAD : (h + 1) * HEAD] for h in range(heads)], 0)
    group = lax.broadcasted_iota(jnp.int32, (heads, 1), 0) // GROUP
    count = kv_ref.shape[2]
    s = jnp.zeros((heads, count), jnp.float32)
    for g in range(heads // GROUP):
        keys = kv_ref[which, 0, :, g * HEAD : (g + 1) * HEAD]
        s = jnp.where(group == g, dot_nt(stacked, keys), s)
    s = jnp.where(lax.broadcasted_iota(jnp.int32, (1, count), 1) < length, s, LOW)
    p = jnp.exp2((s - jnp.max(s, axis=1, keepdims=True)) * SCALE)
    total = jnp.sum(p, axis=1, keepdims=True)
    p = p.astype(jnp.bfloat16)
    mixed = jnp.zeros((heads, HEAD), jnp.float32)
    for g in range(heads // GROUP):
        values = kv_ref[which, 1, :, g * HEAD : (g + 1) * HEAD]
        mixed = jnp.where(group == g, dot_nn(p, values), mixed)
    return (mixed / total).astype(jnp.bfloat16)


def pack_kernel(places, q_near, q_far, kv_near, kv_far, first_ref, second_ref, qkv_ref, near_ref, send_ref, q_out):
    chunk, half, limit = places[0], places[1], places[2]
    rows = q_near.shape[0]
    width = kv_near.shape[2]
    lines = width // HEAD
    q_out[...] = q_far[...]
    row = limit - 1 - (2 * chunk + half) * rows
    shape = (EXTRA // 2, rows)
    here = lax.broadcasted_iota(jnp.int32, shape, 1) == row
    line = lax.broadcasted_iota(jnp.int32, shape, 0)
    labels = lax.broadcasted_iota(jnp.int32, (EXTRA // 2, width), 0)
    queries = []
    for e, ref in enumerate((first_ref, second_ref)):
        length = places[3 + e]
        emb = ref.shape[1]
        heads = emb // HEAD
        hot = lax.broadcasted_iota(jnp.int32, (8, ref.shape[0]), 1) == lax.rem(length - 1, ref.shape[0])
        one = dot_nn(hot.astype(jnp.bfloat16), ref[...])[:1].astype(jnp.bfloat16)
        out = row_attention(one, qkv_ref, e, length, heads)
        spot = lax.broadcasted_iota(jnp.int32, (heads // lines, heads), 1)
        want = lax.broadcasted_iota(jnp.int32, (heads // lines, heads), 0) * lines
        parts = [dot_nn((spot == want + j).astype(jnp.bfloat16), out) for j in range(lines)]
        queries.append(jnp.concatenate(parts, 1))
    queries = jnp.concatenate(queries, 0).astype(jnp.bfloat16)
    for q_ref, kv_ref, out_ref in ((q_near, kv_near, near_ref), (q_far, kv_far, send_ref)):
        out_ref[:rows] = kv_ref[0]
        out_ref[rows : 2 * rows] = kv_ref[1]
        found = jnp.zeros((EXTRA // 2, width), jnp.float32)
        for j in range(q_ref.shape[1] // width):
            hot = (here & (line == j)).astype(jnp.bfloat16)
            found += dot_nn(hot, q_ref[:, j * width : (j + 1) * width])
        for e in range(2):
            found = jnp.where(labels == LABEL + e, places[5 + e].astype(jnp.float32), found)
        out_ref[2 * rows : 2 * rows + EXTRA // 2] = found.astype(jnp.bfloat16)
        out_ref[2 * rows + EXTRA // 2 :] = queries


def pack(places, query, keyval, qry_query, qry_keyval):
    rows, emb = query.shape
    width = keyval.shape[2] // 2
    length = 2 * rows + EXTRA
    step = 16
    near = lambda i, p: (0, p[1])
    far = lambda i, p: (0, 1 - p[1])
    return pl.pallas_call(
        pack_kernel,
        grid_spec=pltpu.PrefetchScalarGridSpec(
            num_scalar_prefetch=1,
            grid=(1,),
            in_specs=[
                pl.BlockSpec((rows, emb // 2), near),
                pl.BlockSpec((rows, emb // 2), far),
                pl.BlockSpec((2, rows, width), lambda i, p: (0, 0, p[1])),
                pl.BlockSpec((2, rows, width), lambda i, p: (0, 0, 1 - p[1])),
                pl.BlockSpec((None, step, emb), lambda i, p: (0, (p[3] - 1) // step, 0)),
                pl.BlockSpec((None, step, emb), lambda i, p: (1, (p[4] - 1) // step, 0)),
                pl.BlockSpec(qry_keyval.shape, lambda i, p: (0, 0, 0, 0)),
            ],
            out_specs=[pl.BlockSpec((length, width), lambda i, p: (0, 0))] * 2
            + [pl.BlockSpec((rows, emb // 2), lambda i, p: (0, 0))],
        ),
        out_shape=[jax.ShapeDtypeStruct((length, width), jnp.bfloat16)] * 2
        + [jax.ShapeDtypeStruct((rows, emb // 2), jnp.bfloat16)],
        compiler_params=pltpu.CompilerParams(vmem_limit_bytes=VMEM),
        name="pack",
    )(places, query, query, keyval, keyval, qry_query, qry_query, qry_keyval)


def doc_kernel(final, hops, only, places, *refs):
    if final:
        q_ref, refs = refs[0], refs[1:]
        piece = jnp.int32(only)
    else:
        own_ref, lent_ref, refs = refs[0], refs[1], refs[2:]
        piece = pl.program_id(1)
    blocks = [(refs[2 * n], refs[2 * n + 1]) for n in range(len(hops))]
    refs = refs[2 * len(hops) :]
    if final:
        o_in, lse_in, o_ref, k_ref, v_ref, spot_ref = refs
    else:
        o_ref, lse_ref, k_ref, v_ref, spot_ref, q_ref = refs
    chunk, half, limit = places[0], places[1], places[2]
    rows = q_ref.shape[0]
    span = 2 * rows
    row_half = jnp.where(piece == 0, half, 1 - half)
    base = chunk * span + row_half * rows

    if not final:

        @pl.when(piece == 0)
        def _():
            q_ref[...] = own_ref[...]

        @pl.when(piece == 1)
        def _():
            q_ref[...] = lent_ref[...]

    v_ref[:, HEAD:] = jnp.ones((v_ref.shape[0], HEAD), jnp.bfloat16)
    lane = lax.broadcasted_iota(jnp.int32, (8, rows), 1)
    count = jnp.int32(0)
    for hop, pair in zip(hops, blocks):
        number = lax.rem(chunk - hop + RING, RING)
        need = (number <= chunk) & (number * span < limit)

        @pl.when(need)
        def _(number=number, pair=pair, count=count):
            for side, block in enumerate(pair):
                start = pl.multiple_of(count * span + side * rows, rows)
                k_ref[pl.ds(start, rows)] = block[:rows]
                v_ref[pl.ds(start, rows), :HEAD] = block[rows : 2 * rows]
                place = half if side == 0 else 1 - half
                spot_ref[:, pl.ds(start, rows)] = lane + number * span + place * rows

        count = count + need.astype(jnp.int32)

    def update(used):
        width = used * span
        edge = base + lax.broadcasted_iota(jnp.int32, (rows, 1), 0)
        mask = spot_ref[:1, :width] <= jnp.minimum(edge, limit - 1)

        def score(h):
            return dot_nt(q_ref[:, h * HEAD : (h + 1) * HEAD], k_ref[:width])

        current = score(0)
        for h in range(GROUP):
            columns = slice(h * HEAD, (h + 1) * HEAD)
            following = score(h + 1) if h + 1 < GROUP else None
            s = jnp.where(mask, current, LOW)
            top = jnp.max(s, axis=1, keepdims=True)
            if final:
                before = lse_in[:, columns]
                high = jnp.maximum(before, top * SCALE)
                p = jnp.exp2(s * SCALE - jnp.concatenate([high] * (width // HEAD), 1))
                mixed = dot_nn(p.astype(jnp.bfloat16), v_ref[:width])
                factor = jnp.exp2(before - high)
                out = (o_in[:, columns].astype(jnp.float32) * factor + mixed[:, :HEAD]) / (
                    factor + mixed[:, HEAD:]
                )
            else:
                p = jnp.exp2((s - top) * SCALE)
                mixed = dot_nn(p.astype(jnp.bfloat16), v_ref[:width])
                total = mixed[:, HEAD:]
                out = mixed[:, :HEAD] / total
                lse_ref[:, columns] = top * SCALE + jnp.log2(total)
            o_ref[:, columns] = out.astype(jnp.bfloat16)
            current = following

    for used in range(1, len(hops) + 1):
        pl.when(count == used)(functools.partial(update, used))

    @pl.when(count == 0)
    def _():
        if final:
            o_ref[...] = o_in[...]
        else:
            o_ref[...] = jnp.zeros_like(o_ref)
            lse_ref[...] = jnp.full_like(lse_ref, LOW)


def doc_part(places, query, lent, blocks, hops, before=None, only=None):
    final = before is not None
    rows, width = lent.shape
    block = GROUP * HEAD
    kv_heads = width // block
    length = blocks[0].shape[0]
    span = 2 * rows * len(hops)
    own_spec = pl.BlockSpec((rows, block), lambda g, i, p: (0, p[1] * kv_heads + g))
    row_spec = pl.BlockSpec((rows, block), lambda g, i, p: (0, g))
    kv_spec = pl.BlockSpec((length, HEAD), lambda g, i, p: (0, g))
    scratch = [
        pltpu.VMEM((span, HEAD), jnp.bfloat16),
        pltpu.VMEM((span, 2 * HEAD), jnp.bfloat16),
        pltpu.VMEM((8, span), jnp.int32),
    ]
    if final:
        piece_spec = pl.BlockSpec((None, rows, block), lambda g, i, p: (only, 0, g))
        spec, rows_in = [(own_spec, query), (row_spec, lent)][only]
        in_specs = [spec] + [kv_spec] * len(blocks) + [piece_spec] * 2
        args = [places, rows_in, *blocks, *before]
        out_specs = spec
        out_shape = jax.ShapeDtypeStruct(rows_in.shape, jnp.bfloat16)
    else:
        piece_spec = pl.BlockSpec((None, rows, block), lambda g, i, p: (i, 0, g))
        in_specs = [own_spec, row_spec] + [kv_spec] * len(blocks)
        args = [places, query, lent, *blocks]
        out_specs = [piece_spec] * 2
        out_shape = [
            jax.ShapeDtypeStruct((2, rows, width), jnp.bfloat16),
            jax.ShapeDtypeStruct((2, rows, width), jnp.float32),
        ]
        scratch.append(pltpu.VMEM((rows, block), jnp.bfloat16))
    pieces = 1 if final else 2
    return pl.pallas_call(
        functools.partial(doc_kernel, final, hops, only),
        grid_spec=pltpu.PrefetchScalarGridSpec(
            num_scalar_prefetch=1,
            grid=(kv_heads, pieces),
            in_specs=in_specs,
            out_specs=out_specs,
            scratch_shapes=scratch,
        ),
        out_shape=out_shape,
        compiler_params=pltpu.CompilerParams(vmem_limit_bytes=VMEM),
        cost_estimate=pl.CostEstimate(
            flops=len(hops) * 4 * pieces * rows * 2 * rows * width,
            bytes_accessed=6 * 2**20,
            transcendentals=2**21,
        ),
        name="doc_part",
    )(*args)


def last_row_kernel(places, *refs):
    blocks, o_ref = refs[:-1], refs[-1]
    chunk, half, limit = places[0], places[1], places[2]
    rows = (blocks[0].shape[0] - EXTRA) // 2
    span = 2 * rows
    lane = lax.broadcasted_iota(jnp.int32, (1, rows), 1)
    spots = []
    query = jnp.zeros((EXTRA // 2, blocks[0].shape[1]), jnp.float32)
    for n, block in enumerate(blocks):
        hop, side = n // 2, n % 2
        number = lax.rem(chunk - hop + RING, RING)
        place = jnp.where(side == 0, half, 1 - half)
        spots.append(lane + number * span + place * rows)
        query += block[2 * rows : 2 * rows + EXTRA // 2].astype(jnp.float32)
    mask = jnp.concatenate(spots, 1) < limit
    lines = query.shape[1] // HEAD
    per = HEADS_HALF // lines
    stacked = jnp.concatenate([query[:per, j * HEAD : (j + 1) * HEAD] for j in range(lines)], 0)
    stacked = stacked.astype(jnp.bfloat16)
    line = lax.rem(lax.broadcasted_iota(jnp.int32, (HEADS_HALF, 1), 0), per)
    groups = HEADS_HALF // GROUP
    group = line // (per // groups)
    scores = jnp.zeros((HEADS_HALF, mask.shape[1]), jnp.float32)
    for g in range(groups):
        keys = jnp.concatenate([b[:rows, g * HEAD : (g + 1) * HEAD] for b in blocks], 0)
        scores = jnp.where(group == g, dot_nt(stacked, keys), scores)
    s = jnp.where(mask, scores, LOW)
    top = jnp.max(s, axis=1, keepdims=True)
    p = jnp.exp2((s - top) * SCALE)
    total = jnp.sum(p, axis=1, keepdims=True)
    weights = p.astype(jnp.bfloat16)
    mixed = jnp.zeros((HEADS_HALF, HEAD), jnp.float32)
    for g in range(groups):
        values = jnp.concatenate([b[rows : 2 * rows, g * HEAD : (g + 1) * HEAD] for b in blocks], 0)
        mixed = jnp.where(group == g, dot_nn(weights, values), mixed)
    out = (mixed / total).astype(jnp.bfloat16).astype(jnp.float32)
    ordered = jnp.concatenate(
        [out[(h % lines) * per + h // lines :][:1] for h in range(HEADS_HALF)], 0
    )
    blank = jnp.zeros_like(ordered)
    o_ref[:HEADS_HALF] = jnp.where(half == 0, ordered, blank)
    o_ref[HEADS_HALF:] = jnp.where(half == 0, blank, ordered)


def last_row(places, blocks):
    whole = pl.BlockSpec(memory_space=pltpu.VMEM)
    return pl.pallas_call(
        last_row_kernel,
        in_specs=[pl.BlockSpec(memory_space=pltpu.SMEM)] + [whole] * len(blocks),
        out_specs=whole,
        out_shape=jax.ShapeDtypeStruct((2 * HEADS_HALF, HEAD), jnp.float32),
        compiler_params=pltpu.CompilerParams(vmem_limit_bytes=VMEM),
        cost_estimate=pl.CostEstimate(flops=2**25, bytes_accessed=4 * 2**20, transcendentals=2**15),
        name="last_row",
    )(places, *blocks)


def contrast_kernel(count, places, d_ref, *refs):
    blocks = refs[:-4]
    qg_ref, part_ref, label_ref, row_ref = refs[-4:]
    high = lax.Precision.HIGHEST
    sources = len(blocks)
    for n, block in enumerate(blocks):
        label_ref[n] = block[: EXTRA // 2].astype(jnp.float32)
        row_ref[n] = block[EXTRA // 2 :].astype(jnp.float32)
    lines = EXTRA // 4
    q = jnp.concatenate(
        [jnp.concatenate([row_ref[:, e * lines + j, :] for j in range(lines)], 1) for e in range(2)], 0
    )
    label = jnp.concatenate([label_ref[:, LABEL + e, :1] for e in range(2)], 0)
    strips = d_ref.shape[1]
    d = jnp.concatenate([d_ref[:, j, :] for j in range(strips)], 1)
    q_scale = lax.rsqrt(jnp.sum(q * q, axis=1, keepdims=True) + 1e-6)
    d_scale = lax.rsqrt(jnp.sum(d * d, axis=1, keepdims=True) + 1e-6)
    qn = q * q_scale
    dn = d * d_scale
    logits = (
        lax.dot_general(
            qn, dn, (((1,), (1,)), ((), ())), preferred_element_type=jnp.float32, precision=high
        )
        / 0.05
    )
    top = jnp.max(logits, axis=1, keepdims=True)
    expo = jnp.exp(logits - top)
    share = expo / jnp.sum(expo, axis=1, keepdims=True)
    docs = lax.broadcasted_iota(jnp.int32, logits.shape, 1).astype(jnp.float32)
    slope = (share - jnp.where(docs == label, 1.0, 0.0)) * (20.0 / count)
    part = dot_tn(slope, qn, high)
    for j in range(strips):
        part_ref[:, j, :] = part[:, j * HEAD : (j + 1) * HEAD]

    def own(x):
        return jnp.concatenate([x[e * sources : e * sources + 1] for e in range(2)], 0)

    q_slope = dot_nn(own(slope), dn, high)
    along = jnp.sum(q_slope * own(qn), axis=1, keepdims=True)
    qg_ref[...] = (q_slope - own(qn) * along) * own(q_scale)


def contrast(count, places, docs, blocks):
    emb = docs.shape[1] * docs.shape[2]
    length, width = blocks[0].shape
    sources = len(blocks)
    extra = pl.BlockSpec((EXTRA, width), lambda i, p: (length // EXTRA - 1, 0))
    return pl.pallas_call(
        functools.partial(contrast_kernel, count),
        grid_spec=pltpu.PrefetchScalarGridSpec(
            num_scalar_prefetch=1,
            grid=(1,),
            in_specs=[pl.BlockSpec(docs.shape, lambda i, p: (0, 0, 0))] + [extra] * sources,
            out_specs=[
                pl.BlockSpec((2, emb), lambda i, p: (0, 0)),
                pl.BlockSpec(docs.shape, lambda i, p: (0, 0, 0)),
            ],
            scratch_shapes=[pltpu.VMEM((sources, EXTRA // 2, width), jnp.float32)] * 2,
        ),
        out_shape=[
            jax.ShapeDtypeStruct((2, emb), jnp.float32),
            jax.ShapeDtypeStruct(docs.shape, jnp.float32),
        ],
        compiler_params=pltpu.CompilerParams(vmem_limit_bytes=VMEM),
        name="contrast",
    )(places, docs, *blocks)


def project_kernel(parts_ref, d_ref, o_ref):
    slope = jnp.sum(parts_ref[...], axis=0)
    d = d_ref[...]

    def whole(x):
        return jnp.sum(jnp.sum(x, axis=1, keepdims=True), axis=0, keepdims=True)

    scale = lax.rsqrt(whole(d * d) + 1e-6)
    dn = d * scale
    out = (slope - dn * whole(slope * dn)) * scale
    for j in range(d.shape[0]):
        o_ref[:, j * HEAD : (j + 1) * HEAD] = out[j : j + 1]


def project(parts, d):
    whole = pl.BlockSpec(memory_space=pltpu.VMEM)
    return pl.pallas_call(
        project_kernel,
        in_specs=[whole] * 2,
        out_specs=whole,
        out_shape=jax.ShapeDtypeStruct((1, d.shape[0] * d.shape[1]), jnp.float32),
        name="project",
    )(parts, d)


def along(array, pairs):
    both = [(2 * s + y, 2 * t + y) for s, t in pairs for y in range(2)]
    return lax.ppermute(array, "seq", both)


def across(array):
    return lax.ppermute(array, "seq", [(i, i ^ 1) for i in range(2 * RING)])


def ring(step):
    return [(s, (s + step) % RING) for s in range(RING)]


def after(array, *earlier):
    return lax.optimization_barrier((array, *earlier))[0]


def shards(doc_query, doc_keyval, qry_query, qry_keyval, doc_len, qry_len, positive):
    emb = doc_query.shape[2]
    seq_count = lax.axis_size("seq")
    doc_count = lax.axis_size("doc")
    seq_index = lax.axis_index("seq")
    half = lax.rem(seq_index, 2)
    half_emb = emb // 2
    own = qry_query.shape[0]
    places = jnp.concatenate(
        [jnp.stack([seq_index // 2, half]).astype(jnp.int32), doc_len, qry_len, positive]
    )
    near, sent, wanted = pack(places, doc_query[0], doc_keyval[0], qry_query, qry_keyval)
    up_near, down_near, up_far, down_far = {0: near}, {0: near}, {}, {}

    def forward(store, step, way, *earlier):
        store[step] = along(after(store[step - 1], *earlier), ring(way))

    def blocks_of(*pairs):
        return [block for pair in pairs for block in pair]

    forward(up_near, 1, 1)
    forward(down_near, 1, -1)
    far = across(sent)
    up_far[0] = down_far[0] = far
    lent = across(wanted)
    qry_out = query_attention(after(qry_len, near), qry_query, qry_keyval, 0, None)
    forward(up_far, 1, 1, qry_out)
    forward(down_far, 1, -1, qry_out)
    forward(up_near, 2, 1, qry_out)
    forward(down_near, 2, -1, qry_out)
    forward(up_far, 2, 1)
    forward(down_far, 2, -1)
    forward(up_near, 3, 1)
    forward(down_near, 3, -1)
    qry_out = query_attention(
        after(qry_len, up_near[2], down_near[2], up_far[1], down_far[1]), qry_query, qry_keyval, 1, qry_out
    )
    forward(up_far, 3, 1, qry_out)
    forward(down_far, 3, -1, qry_out)
    forward(up_near, 4, 1, qry_out)
    early, late = (0, 1, RING - 1, 2, RING - 2), (3, 4, 5)

    def by_hop(n):
        if n == 4:
            return up_near[4], down_far[4]
        return (up_near[n], up_far[n]) if n < 4 else (down_near[RING - n], down_far[RING - n])

    partial = doc_part(
        after(places, up_near[3], down_near[3], up_far[2], down_far[2]),
        doc_query[0],
        lent,
        blocks_of(*(by_hop(n) for n in early)),
        early,
    )
    forward(down_far, 4, -1, partial[0])
    everything = blocks_of(*(by_hop(n) for n in range(RING)))
    row = last_row(after(places, *everything), everything)
    late_blocks = blocks_of(*(by_hop(n) for n in late))
    pooled = row + across(row)
    copies = jnp.broadcast_to(pooled[None], (doc_count, *pooled.shape))
    docs = lax.all_to_all(copies, "doc", 0, 0, tiled=True)
    loan = doc_part(after(places, copies), doc_query[0], lent, late_blocks, late, partial, 1)
    count = float(own * seq_count * doc_count)
    query_grad, part = contrast(count, places, after(docs, loan), everything)
    other = across(after(loan, part))
    parts = lax.all_to_all(part, "doc", 0, 0, tiled=True)
    mine = doc_part(after(places, part), doc_query[0], lent, late_blocks, late, partial, 0)
    parts = after(parts, mine)
    doc_out = lax.dynamic_update_slice_in_dim(mine, other, (1 - half) * half_emb, 1)
    doc_grad = project(parts, pooled)
    return (doc_out[None], qry_out, doc_grad, query_grad)


def solution(mesh):
    placed = (
        P("doc", "seq", None),
        P("doc", None, "seq", None),
        P(("doc", "seq"), None, None),
        P(("doc", "seq"), None, None, None),
        P("doc"),
        P(("doc", "seq")),
        P(("doc", "seq")),
    )
    return jax.shard_map(
        shards,
        mesh=mesh,
        in_specs=placed,
        out_specs=(
            P("doc", "seq", None),
            P(("doc", "seq"), None, None),
            P("doc", None),
            P(("doc", "seq"), None),
        ),
        check_vma=False,
    )
```

```python
import functools
import math

import jax
import jax.numpy as jnp
from jax import lax
from jax.experimental import pallas as pl
from jax.experimental.pallas import tpu as pltpu
from jax.sharding import PartitionSpec as P

HEAD = 128
GROUP = 4
TILE = 256
LOW = -1e30
SCALE = math.log2(math.e) / math.sqrt(HEAD)
VMEM = 60 * 2**20
RING = 8
EXTRA = 32
LABEL = 4
HEADS_HALF = 8


def dot_nt(a, b):
    return lax.dot_general(
        a, b, (((1,), (1,)), ((), ())), preferred_element_type=jnp.float32
    )


def dot_nn(a, b, precision=None):
    return lax.dot_general(
        a, b, (((1,), (0,)), ((), ())), preferred_element_type=jnp.float32, precision=precision
    )


def dot_tn(a, b, precision=None):
    return lax.dot_general(
        a, b, (((0,), (0,)), ((), ())), preferred_element_type=jnp.float32, precision=precision
    )


def query_kernel(index, len_ref, q_ref, kv_ref, *refs):
    o_ref = refs[-1]
    length = len_ref[index]
    count = q_ref.shape[0]
    heads = q_ref.shape[1] // HEAD
    ones = jnp.ones((count, HEAD), jnp.bfloat16)
    items = [(r, h) for r in range(0, count, TILE) for h in range(heads)]

    def score(r, h):
        g = h // GROUP
        q = q_ref[r : r + TILE, h * HEAD : (h + 1) * HEAD]
        return dot_nt(q, kv_ref[0, : r + TILE, g * HEAD : (g + 1) * HEAD])

    current = score(*items[0])
    for i, (r, h) in enumerate(items):
        following = score(*items[i + 1]) if i + 1 < len(items) else None
        width = r + TILE
        g = h // GROUP
        edge = jnp.minimum(r + lax.broadcasted_iota(jnp.int32, (TILE, 1), 0), length - 1)
        mask = lax.broadcasted_iota(jnp.int32, (TILE, width), 1) <= edge
        s = jnp.where(mask, current, LOW)
        top = jnp.max(s, axis=1, keepdims=True)
        p = jnp.exp2((s - top) * SCALE).astype(jnp.bfloat16)
        v = kv_ref[1, :width, g * HEAD : (g + 1) * HEAD]
        mixed = dot_nn(p, jnp.concatenate([v, ones[:width]], 1))
        out = mixed[:, :HEAD] / mixed[:, HEAD:]
        o_ref[r : r + TILE, h * HEAD : (h + 1) * HEAD] = out.astype(jnp.bfloat16)
        current = following


def query_attention(lengths, query, keyval, index, previous):
    _, count, emb = query.shape
    parts = 2
    width = emb // parts
    kv_width = keyval.shape[3] // parts
    in_specs = [
        pl.BlockSpec((None, count, width), lambda j, *_: (index, 0, j)),
        pl.BlockSpec((None, 2, count, kv_width), lambda j, *_: (index, 0, 0, j)),
    ]
    args = [lengths, query, keyval]
    alias = {}
    if previous is not None:
        in_specs.append(pl.BlockSpec(memory_space=pl.ANY))
        args.append(previous)
        alias = {3: 0}
    return pl.pallas_call(
        functools.partial(query_kernel, index),
        grid_spec=pltpu.PrefetchScalarGridSpec(
            num_scalar_prefetch=1,
            grid=(parts,),
            in_specs=in_specs,
            out_specs=pl.BlockSpec((None, count, width), lambda j, *_: (index, 0, j)),
        ),
        out_shape=jax.ShapeDtypeStruct(query.shape, jnp.bfloat16),
        input_output_aliases=alias,
        compiler_params=pltpu.CompilerParams(vmem_limit_bytes=VMEM),
        cost_estimate=pl.CostEstimate(
            flops=4 * count * count * emb, bytes_accessed=5 * 2**20, transcendentals=count * count * 16
        ),
        name="query_attention",
    )(*args)


def row_attention(row, kv_ref, which, length, heads):
    stacked = jnp.concatenate([row[:, h * HEAD : (h + 1) * HEAD] for h in range(heads)], 0)
    group = lax.broadcasted_iota(jnp.int32, (heads, 1), 0) // GROUP
    count = kv_ref.shape[2]
    s = jnp.zeros((heads, count), jnp.float32)
    for g in range(heads // GROUP):
        keys = kv_ref[which, 0, :, g * HEAD : (g + 1) * HEAD]
        s = jnp.where(group == g, dot_nt(stacked, keys), s)
    s = jnp.where(lax.broadcasted_iota(jnp.int32, (1, count), 1) < length, s, LOW)
    p = jnp.exp2((s - jnp.max(s, axis=1, keepdims=True)) * SCALE)
    total = jnp.sum(p, axis=1, keepdims=True)
    p = p.astype(jnp.bfloat16)
    mixed = jnp.zeros((heads, HEAD), jnp.float32)
    for g in range(heads // GROUP):
        values = kv_ref[which, 1, :, g * HEAD : (g + 1) * HEAD]
        mixed = jnp.where(group == g, dot_nn(p, values), mixed)
    return (mixed / total).astype(jnp.bfloat16)


def pack_kernel(places, q_near, q_far, kv_near, kv_far, first_ref, second_ref, qkv_ref, near_ref, send_ref, q_out):
    chunk, half, limit = places[0], places[1], places[2]
    rows = q_near.shape[0]
    width = kv_near.shape[2]
    lines = width // HEAD
    q_out[...] = q_far[...]
    row = limit - 1 - (2 * chunk + half) * rows
    shape = (EXTRA // 2, rows)
    here = lax.broadcasted_iota(jnp.int32, shape, 1) == row
    line = lax.broadcasted_iota(jnp.int32, shape, 0)
    labels = lax.broadcasted_iota(jnp.int32, (EXTRA // 2, width), 0)
    queries = []
    for e, ref in enumerate((first_ref, second_ref)):
        length = places[3 + e]
        emb = ref.shape[1]
        heads = emb // HEAD
        hot = lax.broadcasted_iota(jnp.int32, (8, ref.shape[0]), 1) == lax.rem(length - 1, ref.shape[0])
        one = dot_nn(hot.astype(jnp.bfloat16), ref[...])[:1].astype(jnp.bfloat16)
        out = row_attention(one, qkv_ref, e, length, heads)
        spot = lax.broadcasted_iota(jnp.int32, (heads // lines, heads), 1)
        want = lax.broadcasted_iota(jnp.int32, (heads // lines, heads), 0) * lines
        parts = [dot_nn((spot == want + j).astype(jnp.bfloat16), out) for j in range(lines)]
        queries.append(jnp.concatenate(parts, 1))
    queries = jnp.concatenate(queries, 0).astype(jnp.bfloat16)
    for q_ref, kv_ref, out_ref in ((q_near, kv_near, near_ref), (q_far, kv_far, send_ref)):
        out_ref[:rows] = kv_ref[0]
        out_ref[rows : 2 * rows] = kv_ref[1]
        found = jnp.zeros((EXTRA // 2, width), jnp.float32)
        for j in range(q_ref.shape[1] // width):
            hot = (here & (line == j)).astype(jnp.bfloat16)
            found += dot_nn(hot, q_ref[:, j * width : (j + 1) * width])
        for e in range(2):
            found = jnp.where(labels == LABEL + e, places[5 + e].astype(jnp.float32), found)
        out_ref[2 * rows : 2 * rows + EXTRA // 2] = found.astype(jnp.bfloat16)
        out_ref[2 * rows + EXTRA // 2 :] = queries


def pack(places, query, keyval, qry_query, qry_keyval):
    rows, emb = query.shape
    width = keyval.shape[2] // 2
    length = 2 * rows + EXTRA
    step = 16
    near = lambda i, p: (0, p[1])
    far = lambda i, p: (0, 1 - p[1])
    return pl.pallas_call(
        pack_kernel,
        grid_spec=pltpu.PrefetchScalarGridSpec(
            num_scalar_prefetch=1,
            grid=(1,),
            in_specs=[
                pl.BlockSpec((rows, emb // 2), near),
                pl.BlockSpec((rows, emb // 2), far),
                pl.BlockSpec((2, rows, width), lambda i, p: (0, 0, p[1])),
                pl.BlockSpec((2, rows, width), lambda i, p: (0, 0, 1 - p[1])),
                pl.BlockSpec((None, step, emb), lambda i, p: (0, (p[3] - 1) // step, 0)),
                pl.BlockSpec((None, step, emb), lambda i, p: (1, (p[4] - 1) // step, 0)),
                pl.BlockSpec(qry_keyval.shape, lambda i, p: (0, 0, 0, 0)),
            ],
            out_specs=[pl.BlockSpec((length, width), lambda i, p: (0, 0))] * 2
            + [pl.BlockSpec((rows, emb // 2), lambda i, p: (0, 0))],
        ),
        out_shape=[jax.ShapeDtypeStruct((length, width), jnp.bfloat16)] * 2
        + [jax.ShapeDtypeStruct((rows, emb // 2), jnp.bfloat16)],
        compiler_params=pltpu.CompilerParams(vmem_limit_bytes=VMEM),
        name="pack",
    )(places, query, query, keyval, keyval, qry_query, qry_query, qry_keyval)


def doc_kernel(final, hops, only, places, *refs):
    if final:
        q_ref, refs = refs[0], refs[1:]
        piece = jnp.int32(only)
    else:
        own_ref, lent_ref, refs = refs[0], refs[1], refs[2:]
        piece = pl.program_id(1)
    blocks = [(refs[2 * n], refs[2 * n + 1]) for n in range(len(hops))]
    refs = refs[2 * len(hops) :]
    if final:
        o_in, lse_in, o_ref, k_ref, v_ref, spot_ref = refs
    else:
        o_ref, lse_ref, k_ref, v_ref, spot_ref, q_ref = refs
    chunk, half, limit = places[0], places[1], places[2]
    rows = q_ref.shape[0]
    span = 2 * rows
    row_half = jnp.where(piece == 0, half, 1 - half)
    base = chunk * span + row_half * rows

    if not final:

        @pl.when(piece == 0)
        def _():
            q_ref[...] = own_ref[...]

        @pl.when(piece == 1)
        def _():
            q_ref[...] = lent_ref[...]

    v_ref[:, HEAD:] = jnp.ones((v_ref.shape[0], HEAD), jnp.bfloat16)
    lane = lax.broadcasted_iota(jnp.int32, (8, rows), 1)
    count = jnp.int32(0)
    for hop, pair in zip(hops, blocks):
        number = lax.rem(chunk - hop + RING, RING)
        need = (number <= chunk) & (number * span < limit)

        @pl.when(need)
        def _(number=number, pair=pair, count=count):
            for side, block in enumerate(pair):
                start = pl.multiple_of(count * span + side * rows, rows)
                k_ref[pl.ds(start, rows)] = block[:rows]
                v_ref[pl.ds(start, rows), :HEAD] = block[rows : 2 * rows]
                place = half if side == 0 else 1 - half
                spot_ref[:, pl.ds(start, rows)] = lane + number * span + place * rows

        count = count + need.astype(jnp.int32)

    def update(used):
        width = used * span
        edge = base + lax.broadcasted_iota(jnp.int32, (rows, 1), 0)
        mask = spot_ref[:1, :width] <= jnp.minimum(edge, limit - 1)

        def score(h):
            return dot_nt(q_ref[:, h * HEAD : (h + 1) * HEAD], k_ref[:width])

        current = score(0)
        for h in range(GROUP):
            columns = slice(h * HEAD, (h + 1) * HEAD)
            following = score(h + 1) if h + 1 < GROUP else None
            s = jnp.where(mask, current, LOW)
            top = jnp.max(s, axis=1, keepdims=True)
            if final:
                before = lse_in[:, columns]
                high = jnp.maximum(before, top * SCALE)
                p = jnp.exp2(s * SCALE - jnp.concatenate([high] * (width // HEAD), 1))
                mixed = dot_nn(p.astype(jnp.bfloat16), v_ref[:width])
                factor = jnp.exp2(before - high)
                out = (o_in[:, columns].astype(jnp.float32) * factor + mixed[:, :HEAD]) / (
                    factor + mixed[:, HEAD:]
                )
            else:
                p = jnp.exp2((s - top) * SCALE)
                mixed = dot_nn(p.astype(jnp.bfloat16), v_ref[:width])
                total = mixed[:, HEAD:]
                out = mixed[:, :HEAD] / total
                lse_ref[:, columns] = top * SCALE + jnp.log2(total)
            o_ref[:, columns] = out.astype(jnp.bfloat16)
            current = following

    for used in range(1, len(hops) + 1):
        pl.when(count == used)(functools.partial(update, used))

    @pl.when(count == 0)
    def _():
        if final:
            o_ref[...] = o_in[...]
        else:
            o_ref[...] = jnp.zeros_like(o_ref)
            lse_ref[...] = jnp.full_like(lse_ref, LOW)


def doc_part(places, query, lent, blocks, hops, before=None, only=None):
    final = before is not None
    rows, width = lent.shape
    block = GROUP * HEAD
    kv_heads = width // block
    length = blocks[0].shape[0]
    span = 2 * rows * len(hops)
    own_spec = pl.BlockSpec((rows, block), lambda g, i, p: (0, p[1] * kv_heads + g))
    row_spec = pl.BlockSpec((rows, block), lambda g, i, p: (0, g))
    kv_spec = pl.BlockSpec((length, HEAD), lambda g, i, p: (0, g))
    scratch = [
        pltpu.VMEM((span, HEAD), jnp.bfloat16),
        pltpu.VMEM((span, 2 * HEAD), jnp.bfloat16),
        pltpu.VMEM((8, span), jnp.int32),
    ]
    if final:
        piece_spec = pl.BlockSpec((None, rows, block), lambda g, i, p: (only, 0, g))
        spec, rows_in = [(own_spec, query), (row_spec, lent)][only]
        in_specs = [spec] + [kv_spec] * len(blocks) + [piece_spec] * 2
        args = [places, rows_in, *blocks, *before]
        out_specs = spec
        out_shape = jax.ShapeDtypeStruct(rows_in.shape, jnp.bfloat16)
    else:
        piece_spec = pl.BlockSpec((None, rows, block), lambda g, i, p: (i, 0, g))
        in_specs = [own_spec, row_spec] + [kv_spec] * len(blocks)
        args = [places, query, lent, *blocks]
        out_specs = [piece_spec] * 2
        out_shape = [
            jax.ShapeDtypeStruct((2, rows, width), jnp.bfloat16),
            jax.ShapeDtypeStruct((2, rows, width), jnp.float32),
        ]
        scratch.append(pltpu.VMEM((rows, block), jnp.bfloat16))
    pieces = 1 if final else 2
    return pl.pallas_call(
        functools.partial(doc_kernel, final, hops, only),
        grid_spec=pltpu.PrefetchScalarGridSpec(
            num_scalar_prefetch=1,
            grid=(kv_heads, pieces),
            in_specs=in_specs,
            out_specs=out_specs,
            scratch_shapes=scratch,
        ),
        out_shape=out_shape,
        compiler_params=pltpu.CompilerParams(vmem_limit_bytes=VMEM),
        cost_estimate=pl.CostEstimate(
            flops=len(hops) * 4 * pieces * rows * 2 * rows * width,
            bytes_accessed=6 * 2**20,
            transcendentals=2**21,
        ),
        name="doc_part",
    )(*args)


def last_row_kernel(places, *refs):
    blocks, o_ref = refs[:-1], refs[-1]
    chunk, half, limit = places[0], places[1], places[2]
    rows = (blocks[0].shape[0] - EXTRA) // 2
    span = 2 * rows
    lane = lax.broadcasted_iota(jnp.int32, (1, rows), 1)
    spots = []
    query = jnp.zeros((EXTRA // 2, blocks[0].shape[1]), jnp.float32)
    for n, block in enumerate(blocks):
        hop, side = n // 2, n % 2
        number = lax.rem(chunk - hop + RING, RING)
        place = jnp.where(side == 0, half, 1 - half)
        spots.append(lane + number * span + place * rows)
        query += block[2 * rows : 2 * rows + EXTRA // 2].astype(jnp.float32)
    mask = jnp.concatenate(spots, 1) < limit
    lines = query.shape[1] // HEAD
    per = HEADS_HALF // lines
    stacked = jnp.concatenate([query[:per, j * HEAD : (j + 1) * HEAD] for j in range(lines)], 0)
    stacked = stacked.astype(jnp.bfloat16)
    line = lax.rem(lax.broadcasted_iota(jnp.int32, (HEADS_HALF, 1), 0), per)
    groups = HEADS_HALF // GROUP
    group = line // (per // groups)
    scores = jnp.zeros((HEADS_HALF, mask.shape[1]), jnp.float32)
    for g in range(groups):
        keys = jnp.concatenate([b[:rows, g * HEAD : (g + 1) * HEAD] for b in blocks], 0)
        scores = jnp.where(group == g, dot_nt(stacked, keys), scores)
    s = jnp.where(mask, scores, LOW)
    top = jnp.max(s, axis=1, keepdims=True)
    p = jnp.exp2((s - top) * SCALE)
    total = jnp.sum(p, axis=1, keepdims=True)
    weights = p.astype(jnp.bfloat16)
    mixed = jnp.zeros((HEADS_HALF, HEAD), jnp.float32)
    for g in range(groups):
        values = jnp.concatenate([b[rows : 2 * rows, g * HEAD : (g + 1) * HEAD] for b in blocks], 0)
        mixed = jnp.where(group == g, dot_nn(weights, values), mixed)
    out = (mixed / total).astype(jnp.bfloat16).astype(jnp.float32)
    ordered = jnp.concatenate(
        [out[(h % lines) * per + h // lines :][:1] for h in range(HEADS_HALF)], 0
    )
    blank = jnp.zeros_like(ordered)
    o_ref[:HEADS_HALF] = jnp.where(half == 0, ordered, blank)
    o_ref[HEADS_HALF:] = jnp.where(half == 0, blank, ordered)


def last_row(places, blocks):
    whole = pl.BlockSpec(memory_space=pltpu.VMEM)
    return pl.pallas_call(
        last_row_kernel,
        in_specs=[pl.BlockSpec(memory_space=pltpu.SMEM)] + [whole] * len(blocks),
        out_specs=whole,
        out_shape=jax.ShapeDtypeStruct((2 * HEADS_HALF, HEAD), jnp.float32),
        compiler_params=pltpu.CompilerParams(vmem_limit_bytes=VMEM),
        cost_estimate=pl.CostEstimate(flops=2**25, bytes_accessed=4 * 2**20, transcendentals=2**15),
        name="last_row",
    )(places, *blocks)


def contrast_kernel(count, places, d_ref, *refs):
    blocks = refs[:-4]
    qg_ref, part_ref, label_ref, row_ref = refs[-4:]
    high = lax.Precision.HIGHEST
    sources = len(blocks)
    for n, block in enumerate(blocks):
        label_ref[n] = block[: EXTRA // 2].astype(jnp.float32)
        row_ref[n] = block[EXTRA // 2 :].astype(jnp.float32)
    lines = EXTRA // 4
    q = jnp.concatenate(
        [jnp.concatenate([row_ref[:, e * lines + j, :] for j in range(lines)], 1) for e in range(2)], 0
    )
    label = jnp.concatenate([label_ref[:, LABEL + e, :1] for e in range(2)], 0)
    strips = d_ref.shape[1]
    d = jnp.concatenate([d_ref[:, j, :] for j in range(strips)], 1)
    q_scale = lax.rsqrt(jnp.sum(q * q, axis=1, keepdims=True) + 1e-6)
    d_scale = lax.rsqrt(jnp.sum(d * d, axis=1, keepdims=True) + 1e-6)
    qn = q * q_scale
    dn = d * d_scale
    logits = (
        lax.dot_general(
            qn, dn, (((1,), (1,)), ((), ())), preferred_element_type=jnp.float32, precision=high
        )
        / 0.05
    )
    top = jnp.max(logits, axis=1, keepdims=True)
    expo = jnp.exp(logits - top)
    share = expo / jnp.sum(expo, axis=1, keepdims=True)
    docs = lax.broadcasted_iota(jnp.int32, logits.shape, 1).astype(jnp.float32)
    slope = (share - jnp.where(docs == label, 1.0, 0.0)) * (20.0 / count)
    part = dot_tn(slope, qn, high)
    for j in range(strips):
        part_ref[:, j, :] = part[:, j * HEAD : (j + 1) * HEAD]

    def own(x):
        return jnp.concatenate([x[e * sources : e * sources + 1] for e in range(2)], 0)

    q_slope = dot_nn(own(slope), dn, high)
    along = jnp.sum(q_slope * own(qn), axis=1, keepdims=True)
    qg_ref[...] = (q_slope - own(qn) * along) * own(q_scale)


def contrast(count, places, docs, blocks):
    emb = docs.shape[1] * docs.shape[2]
    length, width = blocks[0].shape
    sources = len(blocks)
    extra = pl.BlockSpec((EXTRA, width), lambda i, p: (length // EXTRA - 1, 0))
    return pl.pallas_call(
        functools.partial(contrast_kernel, count),
        grid_spec=pltpu.PrefetchScalarGridSpec(
            num_scalar_prefetch=1,
            grid=(1,),
            in_specs=[pl.BlockSpec(docs.shape, lambda i, p: (0, 0, 0))] + [extra] * sources,
            out_specs=[
                pl.BlockSpec((2, emb), lambda i, p: (0, 0)),
                pl.BlockSpec(docs.shape, lambda i, p: (0, 0, 0)),
            ],
            scratch_shapes=[pltpu.VMEM((sources, EXTRA // 2, width), jnp.float32)] * 2,
        ),
        out_shape=[
            jax.ShapeDtypeStruct((2, emb), jnp.float32),
            jax.ShapeDtypeStruct(docs.shape, jnp.float32),
        ],
        compiler_params=pltpu.CompilerParams(vmem_limit_bytes=VMEM),
        name="contrast",
    )(places, docs, *blocks)


def project_kernel(parts_ref, d_ref, o_ref):
    slope = jnp.sum(parts_ref[...], axis=0)
    d = d_ref[...]

    def whole(x):
        return jnp.sum(jnp.sum(x, axis=1, keepdims=True), axis=0, keepdims=True)

    scale = lax.rsqrt(whole(d * d) + 1e-6)
    dn = d * scale
    out = (slope - dn * whole(slope * dn)) * scale
    for j in range(d.shape[0]):
        o_ref[:, j * HEAD : (j + 1) * HEAD] = out[j : j + 1]


def project(parts, d):
    whole = pl.BlockSpec(memory_space=pltpu.VMEM)
    return pl.pallas_call(
        project_kernel,
        in_specs=[whole] * 2,
        out_specs=whole,
        out_shape=jax.ShapeDtypeStruct((1, d.shape[0] * d.shape[1]), jnp.float32),
        name="project",
    )(parts, d)


def along(array, pairs):
    both = [(2 * s + y, 2 * t + y) for s, t in pairs for y in range(2)]
    return lax.ppermute(array, "seq", both)


def across(array):
    return lax.ppermute(array, "seq", [(i, i ^ 1) for i in range(2 * RING)])


def ring(step):
    return [(s, (s + step) % RING) for s in range(RING)]


def after(array, *earlier):
    return lax.optimization_barrier((array, *earlier))[0]


def shards(doc_query, doc_keyval, qry_query, qry_keyval, doc_len, qry_len, positive):
    emb = doc_query.shape[2]
    seq_count = lax.axis_size("seq")
    doc_count = lax.axis_size("doc")
    seq_index = lax.axis_index("seq")
    half = lax.rem(seq_index, 2)
    half_emb = emb // 2
    own = qry_query.shape[0]
    places = jnp.concatenate(
        [jnp.stack([seq_index // 2, half]).astype(jnp.int32), doc_len, qry_len, positive]
    )
    near, sent, wanted = pack(places, doc_query[0], doc_keyval[0], qry_query, qry_keyval)
    up_near, down_near, up_far, down_far = {0: near}, {0: near}, {}, {}

    def forward(store, step, way, *earlier):
        store[step] = along(after(store[step - 1], *earlier), ring(way))

    def blocks_of(*pairs):
        return [block for pair in pairs for block in pair]

    forward(up_near, 1, 1)
    forward(down_near, 1, -1)
    far = across(sent)
    up_far[0] = down_far[0] = far
    parted = half_emb // 2
    lent = jnp.concatenate([across(wanted[:, :parted]), across(wanted[:, parted:])], 1)
    qry_out = query_attention(after(qry_len, near), qry_query, qry_keyval, 0, None)
    forward(up_far, 1, 1, qry_out)
    forward(down_far, 1, -1, qry_out)
    forward(up_near, 2, 1, qry_out)
    forward(down_near, 2, -1, qry_out)
    forward(up_far, 2, 1)
    forward(down_far, 2, -1)
    forward(up_near, 3, 1)
    forward(down_near, 3, -1)
    qry_out = query_attention(
        after(qry_len, up_near[2], down_near[2], up_far[1], down_far[1]), qry_query, qry_keyval, 1, qry_out
    )
    forward(up_far, 3, 1, qry_out)
    forward(down_far, 3, -1, qry_out)
    forward(up_near, 4, 1, qry_out)
    early, late = (0, 1, RING - 1, 2, RING - 2), (3, 4, 5)

    def by_hop(n):
        if n == 4:
            return up_near[4], down_far[4]
        return (up_near[n], up_far[n]) if n < 4 else (down_near[RING - n], down_far[RING - n])

    partial = doc_part(
        after(places, up_near[3], down_near[3], up_far[2], down_far[2]),
        doc_query[0],
        lent,
        blocks_of(*(by_hop(n) for n in early)),
        early,
    )
    forward(down_far, 4, -1, partial[0])
    everything = blocks_of(*(by_hop(n) for n in range(RING)))
    row = last_row(after(places, *everything), everything)
    late_blocks = blocks_of(*(by_hop(n) for n in late))
    pooled = row + across(row)
    copies = jnp.broadcast_to(pooled[None], (doc_count, *pooled.shape))
    docs = lax.all_to_all(copies, "doc", 0, 0, tiled=True)
    loan = doc_part(after(places, copies), doc_query[0], lent, late_blocks, late, partial, 1)
    count = float(own * seq_count * doc_count)
    query_grad, part = contrast(count, places, after(docs, loan), everything)
    other = across(after(loan, part))
    parts = lax.all_to_all(part, "doc", 0, 0, tiled=True)
    mine = doc_part(after(places, part), doc_query[0], lent, late_blocks, late, partial, 0)
    parts = after(parts, mine)
    doc_out = lax.dynamic_update_slice_in_dim(mine, other, (1 - half) * half_emb, 1)
    doc_grad = project(parts, pooled)
    return (doc_out[None], qry_out, doc_grad, query_grad)


def solution(mesh):
    placed = (
        P("doc", "seq", None),
        P("doc", None, "seq", None),
        P(("doc", "seq"), None, None),
        P(("doc", "seq"), None, None, None),
        P("doc"),
        P(("doc", "seq")),
        P(("doc", "seq")),
    )
    return jax.shard_map(
        shards,
        mesh=mesh,
        in_specs=placed,
        out_specs=(
            P("doc", "seq", None),
            P(("doc", "seq"), None, None),
            P("doc", None),
            P(("doc", "seq"), None),
        ),
        check_vma=False,
    )
```
